512 devices in a mesh: dp: 8 (over x, core), tm: 16 (over z), space: 4 (over y).
Axes of the slice: x: 4, y: 4, z: 16, core: 2. Of those that a mesh axis runs over, the one named last changes fastest.
Arguments:
- groups: bfloat16 [512, 1, 96, 16, 128], P(('dp', 'tm'), None, None, 'space'), may hold values from -6 to 6
- plan_owner: int32 [8, 64], P('dp'), may hold values from 0 to 15, as said below
- plan_slot: int32 [8, 64], P('dp'), may hold values from 0 to 3, as said below
- clip_lengths: int32 [12], replicated, may hold values from 1 to 81, 512 in all
- gain_one: float32 [96], replicated, may hold values from 0.25 to 1.75
- weight_one: bfloat16 [3, 3, 3, 96, 96], replicated, may hold values from -0.125 to 0.125
- bias_one: float32 [96], replicated, may hold values from -3 to 3
- gain_two: float32 [96], replicated, may hold values from 0.25 to 1.75
- weight_two: bfloat16 [3, 3, 3, 96, 96], replicated, may hold values from -0.125 to 0.125
- bias_two: float32 [96], replicated, may hold values from -2 to 2
Outputs:
- encoded: bfloat16 [512, 96, 16, 128], P(('dp', 'tm'), None, 'space')
The draws below stay inside these ranges and needn't reach their ends.
Inputs may be any that keep to these rules, and one draw needn't show every extreme that they name: `plan_owner`: in each span every loader (index l along tm, entries l * 4 to l * 4 + 3) sends either none or exactly 1 of its groups to an owner, and every owner receives 4 groups. Within a span the pairs (plan_owner, plan_slot) of its groups are all different. `clip_lengths`: the lengths sum to 512; a clip may be as short as one frame.
All inputs are finite; a program needn't handle non-finite values.
Results may differ from the reference program's by a relative error of at most 0.0037.
Values may be sent and summed in bfloat16 or wider, within the bound.
A program may use at most 64 MiB of HBM per device.

```python
import math
import jax
import jax.numpy as jnp
import numpy as np
from jax import lax

C = 96
GROUP_FR = 1
COLS = 128
CH_DEV = 4
GROUPS = 512
FRAMES = 512
ROWS = 16
CLIPS = 12
CLIP_MAX = 81
N_DP = 8
N_TM = 16


def span_plan(key):
    count = min(CH_DEV, N_TM)
    keys = jax.random.split(key, 5)
    shifts = jax.random.permutation(keys[0], N_TM)[:count]
    outer = jax.random.permutation(keys[1], N_TM)
    inner = jax.random.permutation(keys[2], N_TM)
    arrival = jax.vmap(lambda k: jax.random.permutation(k, CH_DEV))(jax.random.split(keys[3], N_TM))
    owner = outer[(inner[:, None] + shifts[arrival % count]) % N_TM]
    places = jax.vmap(lambda k: jax.random.permutation(k, CH_DEV))(jax.random.split(keys[4], N_TM))
    slot = places[owner, arrival]
    return (owner.reshape(-1).astype(jnp.int32), slot.reshape(-1).astype(jnp.int32))


def build_plan(key):
    return jax.vmap(span_plan)(jax.random.split(key, N_DP))


def draw_plan_owner(key, part):
    owner, slot = build_plan(key)
    return owner


def draw_plan_slot(key, part):
    owner, slot = build_plan(key)
    return slot


def steps_of(own_key, dims, cuts, smallest, top_value):
    level, own = 1.0, jax.random.fold_in(own_key, 6)
    for axis_at, shards_of in cuts:
        draws = jnp.exp(jax.random.uniform(jax.random.fold_in(own, axis_at), (shards_of,), jnp.float32, smallest / len(cuts), top_value / len(cuts)))
        level = level * jnp.repeat(draws, dims[axis_at] // shards_of).reshape([-1 if axis == axis_at else 1 for axis in range(len(dims))])
    return level


def split_up(number_of, total, most, lean):
    weights = [(1 << 20) // math.isqrt(grade ** lean) + 1 for grade in range(2, number_of + 1)]
    spare, given = total - most - (number_of - 1), [1] * (number_of - 1)
    while spare > 0:
        candidates = [i for i in range(number_of - 1) if given[i] < most]
        whole, left = sum([weights[i] for i in candidates]), spare
        for i in candidates:
            addition = min(most - given[i], max(1, left * weights[i] // whole), spare)
            given[i] = given[i] + addition
            spare = spare - addition
    return np.array([most] + given)


def uneven_parts(stream_key, amount, total, limit, lean):
    if amount == 2:
        one = jax.random.randint(stream_key, (), max(1, total - limit), min(limit, total - 1) + 1)
        return jnp.stack([one, total - one])
    tallies = jnp.asarray(split_up(amount, total, limit, lean), jnp.int32)
    twos = (amount - 1) // 2
    donor, sink = tallies[1:1 + 2 * twos:2], tallies[2:2 + 2 * twos:2]
    margin = jnp.minimum(donor - 1, limit - sink)
    passed = jax.random.randint(jax.random.fold_in(stream_key, 1), (twos,), 0, 1 << 20) % (margin + 1)
    tallies = tallies.at[1:1 + 2 * twos:2].set(donor - passed).at[2:2 + 2 * twos:2].set(sink + passed)
    return tallies[jax.random.permutation(jax.random.fold_in(stream_key, 2), amount)]


def gaussian(own_key, extent, deviation, reach, cuts=(), held_as=jnp.bfloat16):
    level = steps_of(own_key, extent, cuts, -0.22, 0.18) if cuts else 1.0
    drawn = jax.random.normal(own_key, extent, jnp.float32) * deviation * level
    return jnp.minimum(jnp.maximum(drawn, -reach), reach).astype(held_as)


def setup_inputs(seed: int = 0) -> dict:
    key_list = jax.random.split(jax.random.key(seed), 11)
    return {
        "groups": gaussian(key_list[0], (GROUPS, GROUP_FR, C, ROWS, COLS), 1.0, 6.0, ((0, 128), (3, 4))),
        "plan_owner": draw_plan_owner(jax.random.fold_in(key_list[10], 71), 0),
        "plan_slot": draw_plan_slot(jax.random.fold_in(key_list[10], 71), 0),
        "clip_lengths": uneven_parts(key_list[3], CLIPS, FRAMES, CLIP_MAX, 0).astype(jnp.int32),
        "gain_one": jnp.clip(1.0 + 0.15 * jax.random.normal(key_list[4], (C,), jnp.float32), 0.25, 1.75),
        "weight_one": gaussian(key_list[5], (3, 3, 3, C, C), (27 * C) ** -0.5, 0.125),
        "bias_one": gaussian(key_list[6], (C,), 0.5, 3.0, (), jnp.float32),
        "gain_two": jnp.clip(1.0 + 0.15 * jax.random.normal(key_list[7], (C,), jnp.float32), 0.25, 1.75),
        "weight_two": gaussian(key_list[8], (3, 3, 3, C, C), (27 * C) ** -0.5, 0.125),
        "bias_two": gaussian(key_list[9], (C,), 0.3, 2.0, (), jnp.float32),
    }


def normed_silu(values, gain):
    square = lax.optimization_barrier(jnp.mean(values * values, axis=1, keepdims=True))
    return jax.nn.silu(values * lax.rsqrt(square + 1e-06) * gain[None, :, None, None])

def clip_offsets(frame_ids, clip_lengths):
    starts = (jnp.cumsum(clip_lengths) - clip_lengths).astype(jnp.int32)
    below = starts[None, :] <= frame_ids[:, None]
    latest = lax.optimization_barrier(jnp.max(jnp.where(below, starts[None, :], 0), axis=1)).astype(jnp.int32)
    return frame_ids - latest

def causal_conv(field, weight, keep):
    frames = field.shape[0] - 2
    rows = field.shape[2]
    cols = field.shape[3]
    padded = jnp.pad(field, ((0, 0), (0, 0), (1, 1), (1, 1))).astype(jnp.float32)
    total = jnp.zeros((frames, field.shape[1], rows, cols), jnp.float32)
    for back in range(3):
        tap = 2 - back
        part = jnp.zeros_like(total)
        for drow in range(3):
            for dcol in range(3):
                window = padded[tap:tap + frames, :, drow:drow + rows, dcol:dcol + cols]
                part = part + jnp.einsum('oi,firw->forw', weight[tap, drow, dcol].astype(jnp.float32), window)
        total = total + keep[:, back][:, None, None, None] * part
    return total

def reference(groups, plan_owner, plan_slot, clip_lengths, gain_one, weight_one, bias_one, gain_two, weight_two, bias_two):
    places = (jnp.arange(N_DP, dtype=jnp.int32)[:, None] * N_TM + plan_owner) * CH_DEV + plan_slot
    placed = jnp.zeros_like(groups).at[places.reshape(-1).astype(jnp.int32)].set(groups)
    timeline = placed.reshape(FRAMES, C, ROWS, COLS)
    padded = jnp.concatenate([jnp.zeros((4, C, ROWS, COLS), timeline.dtype), timeline], axis=0)
    span_frames = N_TM * CH_DEV * GROUP_FR

    def one_span(index):
        first = (index * span_frames).astype(jnp.int32)
        block = lax.dynamic_slice_in_dim(padded, first, span_frames + 4, 0)
        frame_ids = first - 4 + jnp.arange(span_frames + 4, dtype=jnp.int32)
        offsets = clip_offsets(frame_ids, clip_lengths)
        keep = (offsets[:, None] >= jnp.arange(3, dtype=jnp.int32)[None, :]).astype(jnp.float32)
        hidden_one = normed_silu(block.astype(jnp.float32), gain_one).astype(jnp.bfloat16)
        act = causal_conv(hidden_one, weight_one, keep[2:]) + bias_one[None, :, None, None]
        hidden_two = normed_silu(act, gain_two).astype(jnp.bfloat16)
        mixed = causal_conv(hidden_two, weight_two, keep[4:]) + bias_two[None, :, None, None]
        return (block[4:].astype(jnp.float32) + mixed).astype(jnp.bfloat16)
    spans = lax.map(one_span, jnp.arange(N_DP, dtype=jnp.int32))
    return spans.reshape(FRAMES, C, ROWS, COLS)
```

```python
import jax
import jax.numpy as jnp
from jax import lax
from jax.experimental import pallas as pl
from jax.experimental.pallas import tpu as pltpu
from jax.sharding import PartitionSpec as P

MESH = pl.DeviceIdType.MESH
STEPS = 14
PARTS = 2


def shifted(value, axis, steps):
    count = lax.axis_size(axis)
    initial, last = (max(0, -steps), min(count, count - steps))
    return lax.ppermute(value, axis, [(source, source + steps) for source in range(initial, last)])


def with_halo(block, sides, width):
    for axis, dim in sides:
        count = lax.axis_size(axis)
        forward = [(i, i + 1) for i in range(count - 1)]
        backward = [(target, source) for source, target in forward]
        low = lax.ppermute(
            lax.slice_in_dim(block, block.shape[dim] - width, None, axis=dim), axis, forward
        )
        high = lax.ppermute(lax.slice_in_dim(block, 0, width, axis=dim), axis, backward)
        block = jnp.concatenate([low, block, high], axis=dim)
    return block


def normed_silu(values, gain):
    square = jnp.mean(values * values, axis=1, keepdims=True)
    return jax.nn.silu(values * lax.rsqrt(square + 1e-06) * gain[None, :, None, None])


def frame_offsets(frame_ids, clip_lengths):
    starts = jnp.cumsum(clip_lengths) - clip_lengths
    below = starts[None, :] <= frame_ids[:, None]
    latest = jnp.max(jnp.where(below, starts[None, :], 0), axis=1)
    return frame_ids - latest


def causal_conv(field, weight, keep):
    frames = field.shape[0] - 2
    width = field.shape[1]
    rows = field.shape[2] - 2
    cols = field.shape[3]
    padded = jnp.pad(field, ((0, 0), (0, 0), (0, 0), (1, 1)))
    layers = [
        padded[tap : tap + frames] * keep[:, 2 - tap][:, None, None, None] for tap in range(3)
    ]
    stacked = jnp.stack(layers, axis=1).reshape(frames, 3 * width, rows + 2, cols + 2)
    kernel = jnp.transpose(weight, (1, 2, 3, 0, 4)).reshape(3, 3, width, 3 * width)
    total = jnp.zeros((frames, width, rows, cols), jnp.float32)
    for drow in range(3):
        for dcol in range(3):
            window = stacked[:, :, drow : drow + rows, dcol : dcol + cols]
            total = total + jnp.einsum(
                "ok,fkrw->forw", kernel[drow, dcol], window, preferred_element_type=jnp.float32
            )
    return total


def general_body(
    groups,
    plan_owner,
    plan_slot,
    clip_lengths,
    gain_one,
    weight_one,
    bias_one,
    gain_two,
    weight_two,
    bias_two,
):
    owners_count = lax.axis_size("tm")
    place = lax.axis_index("tm")
    span_index = lax.axis_index("dp")
    per_dev = groups.shape[0]
    capacity = max(1, per_dev // owners_count)
    frames = per_dev * groups.shape[1]
    width = groups.shape[2]
    rows = groups.shape[3]
    cols = groups.shape[4]
    owners_all = plan_owner[0].reshape(owners_count, per_dev)
    slots_all = plan_slot[0].reshape(owners_count, per_dev)
    earlier = jnp.arange(per_dev)[:, None] > jnp.arange(per_dev)[None, :]
    same_owner = owners_all[:, :, None] == owners_all[:, None, :]
    ranks = jnp.sum(same_owner & earlier[None], axis=2)
    mine_owner = lax.dynamic_index_in_dim(owners_all, place, 0, keepdims=False)
    mine_rank = lax.dynamic_index_in_dim(ranks, place, 0, keepdims=False)
    targets = jnp.arange(owners_count, dtype=jnp.int32)[:, None, None]
    copies = jnp.arange(capacity, dtype=jnp.int32)[None, :, None]
    select = (mine_owner[None, None, :] == targets) & (mine_rank[None, None, :] == copies)
    select = select.astype(jnp.bfloat16).reshape(owners_count * capacity, per_dev)
    outgoing = jnp.dot(select, groups.reshape(per_dev, -1), preferred_element_type=jnp.float32)
    outgoing = outgoing.astype(jnp.bfloat16).reshape((owners_count * capacity,) + groups.shape[1:])
    incoming = lax.all_to_all(outgoing, "tm", split_axis=0, concat_axis=0, tiled=True)
    slot_ids = jnp.arange(per_dev, dtype=jnp.int32)[:, None, None, None]
    copy_ids = jnp.arange(capacity, dtype=jnp.int32)[None, None, :, None]
    pick = (
        (owners_all == place)[None, :, None, :]
        & (slots_all[None, :, None, :] == slot_ids)
        & (ranks[None, :, None, :] == copy_ids)
    )
    pick = (
        jnp.sum(pick.astype(jnp.int32), axis=3)
        .astype(jnp.bfloat16)
        .reshape(per_dev, owners_count * capacity)
    )
    local = jnp.dot(
        pick, incoming.reshape(owners_count * capacity, -1), preferred_element_type=jnp.float32
    )
    local = local.astype(jnp.bfloat16).reshape(frames, width, rows, cols)
    first = (span_index * owners_count + place) * frames
    frame_ids = first - 4 + jnp.arange(frames + 4, dtype=jnp.int32)
    offsets = frame_offsets(frame_ids, clip_lengths)
    keep = (offsets[:, None] >= jnp.arange(3, dtype=jnp.int32)[None, :]).astype(jnp.bfloat16)
    residual = local.astype(jnp.float32)
    hidden_one = normed_silu(residual, gain_one).astype(jnp.bfloat16)
    cache_first = shifted(hidden_one[frames - 2 :], ("dp", "tm"), 1)
    banded_one = with_halo(jnp.concatenate([cache_first, hidden_one], axis=0), (("space", 2),), 1)
    act = causal_conv(banded_one, weight_one, keep[4:]) + bias_one[None, :, None, None]
    hidden_two = normed_silu(act, gain_two).astype(jnp.bfloat16)
    cache_second = shifted(hidden_two[frames - 2 :], ("dp", "tm"), 1)
    banded_two = with_halo(jnp.concatenate([cache_second, hidden_two], axis=0), (("space", 2),), 1)
    mixed = causal_conv(banded_two, weight_two, keep[4:])
    return (residual + mixed + bias_two[None, :, None, None]).astype(jnp.bfloat16)


def column(row, size):
    down = lax.broadcasted_iota(jnp.int32, (size, size), 0)
    across = lax.broadcasted_iota(jnp.int32, (size, size), 1)
    spread = jnp.where(down == across, jnp.broadcast_to(row, (size, size)), jnp.zeros((), row.dtype))
    return jnp.sum(spread, axis=1, keepdims=True)


def plan_schedule(owner_ref, slot_ref, sched, count, per_dev):
    total = count * per_dev
    shape = (total, 128)
    frame = lax.broadcasted_iota(jnp.int32, shape, 0)
    lane = lax.broadcasted_iota(jnp.int32, shape, 1) & (count - 1)
    owner = jnp.broadcast_to(column(owner_ref[...], total), shape)
    place = jnp.broadcast_to(column(slot_ref[...], total), shape)
    source = frame // per_dev
    entry = frame - source * per_dev
    ahead = (owner - source) & (count - 1)
    half = count // 2
    forward = (ahead < half) | ((ahead == half) & ((source & 1) == 0))
    here = lane == source
    code = (frame << 10) | (place << 8) | entry
    right = jnp.where(here & forward & (ahead > 0), (ahead << 16) | code, 0)
    left = jnp.where(here & jnp.logical_not(forward), ((count - ahead) << 16) | code, 0)
    final = tuple(
        jnp.max(jnp.where(here & (ahead == 0) & (place == s), entry, 0), axis=0, keepdims=True)
        for s in range(per_dev)
    )

    def one(t, way, state, final):
        best = jnp.max(state, axis=0, keepdims=True)
        sched[pl.ds(2 * t + way, 1), :] = best & 255
        state = jnp.where(state == best, 0, state)
        entry = per_dev + 2 * t + way
        moved = jnp.where(best > 0, best - (best & 255) - (1 << 16) + entry, -1)
        moved = pltpu.roll(moved, 1 if way == 0 else 127, 1)
        there = (moved >= 0) & (moved < (1 << 16))
        final = tuple(
            jnp.where(there & (((moved >> 8) & 3) == s), entry, final[s]) for s in range(per_dev)
        )
        state = jnp.where((frame == ((moved >> 10) & 63)) & (moved >= (1 << 16)), moved, state)
        return state, final

    def step(t, carry):
        right, left, final = carry
        right, final = one(t, 0, right, final)
        left, final = one(t, 1, left, final)
        return right, left, final

    right, left, final = lax.fori_loop(0, STEPS, step, (right, left, final))
    for s in range(per_dev):
        sched[pl.ds(2 * STEPS + s, 1), :] = final[s]
    late = jnp.max(jnp.maximum(right, left), axis=0, keepdims=True)
    late = jnp.max(late, axis=1, keepdims=True)
    return (late > 0).astype(jnp.float32)


def silu_norm(values, gain):
    square = jnp.mean(values * values, axis=0, keepdims=True)
    scaled = values * lax.rsqrt(square + 1e-06) * gain
    return scaled / (1.0 + jnp.exp(-scaled))


def conv_rows(field, weights, mask, at, rows):
    ch, cols = field.shape[2], field.shape[3]
    right_side = jnp.concatenate(
        [field[at : at + 3, r : r + 3].reshape(9 * ch, cols) for r in range(rows)], axis=1
    )
    sums = jnp.dot(weights * mask, right_side, preferred_element_type=jnp.float32)
    lane = lax.broadcasted_iota(jnp.int32, (ch, cols), 1)
    out = []
    for r in range(rows):
        part = sums[:, r * cols : (r + 1) * cols]
        low = jnp.where(lane == 0, 0.0, pltpu.roll(part[:ch], 1, 1))
        high = jnp.where(lane == cols - 1, 0.0, pltpu.roll(part[2 * ch :], cols - 1, 1))
        out.append(part[ch : 2 * ch] + low + high)
    return out


def block_kernel(
    groups, owner, slot, clips, gain_one, weight_one, bias_one, gain_two, weight_two, bias_two,
    out, late_out,
    pool, sending, arrived, sched, sched_s, h_one, h_two, timeline, late_all,
    send_sem, recv_sem, sched_sem, halo_send, halo_recv, late_send, late_recv,
):
    spans, places, bands = lax.axis_size("dp"), lax.axis_size("tm"), lax.axis_size("space")
    dp, tm, sp = lax.axis_index("dp"), lax.axis_index("tm"), lax.axis_index("space")
    per_dev, rows, ch, cols = out.shape
    part_rows = rows * ch // PARTS
    tm_up, tm_down = lax.rem(tm + 1, places), lax.rem(tm + places - 1, places)
    sp_up, sp_down = lax.rem(sp + 1, bands), lax.rem(sp + bands - 1, bands)
    dp_up, dp_down = lax.rem(dp + 1, spans), lax.rem(dp + spans - 1, spans)
    dp_next = jnp.where(tm == places - 1, dp_up, dp)
    dp_prev = jnp.where(tm == 0, dp_down, dp)

    barrier = pltpu.get_barrier_semaphore()
    friends = [(dp, tm_up, sp), (dp, tm_down, sp), (dp, tm, sp_up), (dp, tm, sp_down)]
    friends += [(dp_next, tm_up, s) for s in (sp, sp_up, sp_down)]
    friends += [(dp_prev, tm_down, s) for s in (sp, sp_up, sp_down)]
    friends += [(lax.rem(dp + k, spans), tm, sp) for k in range(1, 8)]
    for friend in friends:
        pl.semaphore_signal(barrier, inc=1, device_id=friend, device_id_type=MESH)

    late = plan_schedule(owner, slot, sched, places, per_dev)
    late_all[0] = jnp.broadcast_to(late, (8, 128))
    to_scalars = pltpu.make_async_copy(sched, sched_s, sched_sem)
    to_scalars.start()
    for f in range(per_dev):
        for p in range(PARTS):
            pool[f, p] = groups[f, p * part_rows : (p + 1) * part_rows]
    to_scalars.wait()
    pl.semaphore_wait(barrier, len(friends))

    late_copies = []
    for k in range(1, 8):
        copy = pltpu.make_async_remote_copy(
            src_ref=late_all.at[0], dst_ref=late_all.at[k], send_sem=late_send.at[k - 1],
            recv_sem=late_recv.at[k - 1], device_id=(lax.rem(dp + k, spans), tm, sp), device_id_type=MESH,
        )
        copy.start()
        late_copies.append(copy)

    def hop(t, way, p):
        return pltpu.make_async_remote_copy(
            src_ref=sending.at[t, way, p], dst_ref=arrived.at[t, way, p],
            send_sem=send_sem.at[t, way, p], recv_sem=recv_sem.at[t, way, p],
            device_id=(dp, tm_up if way == 0 else tm_down, sp), device_id_type=MESH,
        )

    def send(t, p):
        for way in range(2):
            sending[t, way, p] = pool[sched_s[2 * t + way, tm], p]
            hop(t, way, p).start()

    def receive(t, p):
        for way in range(2):
            hop(t, way, p).wait()
            pool[per_dev + 2 * t + way, p] = arrived[t, way, p]

    for p in range(PARTS):
        send(0, p)

    def step(t, carry):
        for p in range(PARTS):
            receive(t - 1, p)
            send(t, p)
        return carry

    lax.fori_loop(1, STEPS, step, 0)
    for p in range(PARTS):
        receive(STEPS - 1, p)

    gain_a = column(gain_one[...], ch)
    gain_b = column(gain_two[...], ch)
    bias_a = column(bias_one[...], ch)
    bias_b = column(bias_two[...], ch)
    first = (dp * places + tm) * per_dev
    offsets = []
    for s in range(per_dev):
        start, latest = jnp.int32(0), jnp.int32(0)
        for c in range(clips.shape[1]):
            latest = jnp.where(start <= first + s, start, latest)
            start = start + clips[0, c]
        offsets.append(first + s - latest)
    tap = lax.broadcasted_iota(jnp.int32, (1, 9 * ch), 1) // (3 * ch)
    masks = [(2 - tap <= offsets[s]).astype(jnp.float32).astype(jnp.bfloat16) for s in range(per_dev)]

    for s in range(per_dev):
        entry = sched_s[2 * STEPS + s, tm]
        for p in range(PARTS):
            timeline[s, p] = pool[entry, p]
        for r in range(rows):
            p, at = divmod(r * ch, part_rows)
            values = timeline[s, p, at : at + ch].astype(jnp.float32)
            h_one[2 + s, 1 + r] = silu_norm(values, gain_a).astype(jnp.bfloat16)

    def exchange(field, turn):
        copies = []
        for k, (src, dst, device) in enumerate((
            (field.at[4:6, 1:5], field.at[0:2, 1:5], (dp_next, tm_up, sp)),
            (field.at[2:6, 4], field.at[2:6, 0], (dp, tm, sp_up)),
            (field.at[2:6, 1], field.at[2:6, 5], (dp, tm, sp_down)),
            (field.at[4:6, 4], field.at[0:2, 0], (dp_next, tm_up, sp_up)),
            (field.at[4:6, 1], field.at[0:2, 5], (dp_next, tm_up, sp_down)),
        )):
            copy = pltpu.make_async_remote_copy(
                src_ref=src, dst_ref=dst, send_sem=halo_send.at[turn, k], recv_sem=halo_recv.at[turn, k],
                device_id=device, device_id_type=MESH,
            )
            copy.start()
            copies.append(copy)
        for copy in copies:
            copy.wait()

        @pl.when(sp == 0)
        def _():
            field[:, 0] = jnp.zeros((per_dev + 2, ch, cols), field.dtype)

        @pl.when(sp == bands - 1)
        def _():
            field[:, rows + 1] = jnp.zeros((per_dev + 2, ch, cols), field.dtype)

    exchange(h_one, 0)
    for s in range(per_dev):
        for r, act in enumerate(conv_rows(h_one, weight_one[...], masks[s], s, rows)):
            h_two[2 + s, 1 + r] = silu_norm(act + bias_a, gain_b).astype(jnp.bfloat16)
    exchange(h_two, 1)
    for s in range(per_dev):
        for r, mixed in enumerate(conv_rows(h_two, weight_two[...], masks[s], s, rows)):
            p, at = divmod(r * ch, part_rows)
            kept = timeline[s, p, at : at + ch].astype(jnp.float32)
            out[s, r] = (kept + mixed + bias_b).astype(jnp.bfloat16)

    for copy in late_copies:
        copy.wait()
    late_out[...] = jnp.max(late_all[...], axis=0)


def body(
    groups, plan_owner, plan_slot, clip_lengths, gain_one, weight_one, bias_one, gain_two, weight_two, bias_two
):
    per_dev, _, ch, rows, cols = groups.shape
    turned = jnp.transpose(groups[:, 0], (0, 2, 1, 3)).reshape(per_dev, rows * ch, cols)
    weights = [
        jnp.transpose(w, (2, 3, 0, 1, 4)).reshape(3 * ch, 9 * ch) for w in (weight_one, weight_two)
    ]
    vmem, smem = pl.BlockSpec(memory_space=pltpu.VMEM), pl.BlockSpec(memory_space=pltpu.SMEM)
    part = (PARTS, rows * ch // PARTS, cols)
    sched_rows = (2 * STEPS + per_dev + 7) // 8 * 8
    fast, late = pl.pallas_call(
        block_kernel,
        out_shape=(
            jax.ShapeDtypeStruct((per_dev, rows, ch, cols), jnp.bfloat16),
            jax.ShapeDtypeStruct((8, 128), jnp.float32),
        ),
        in_specs=[vmem, vmem, vmem, smem] + [vmem] * 6,
        out_specs=(vmem, vmem),
        scratch_shapes=[
            pltpu.VMEM((per_dev + 2 * STEPS,) + part, jnp.bfloat16),
            pltpu.VMEM((STEPS, 2) + part, jnp.bfloat16),
            pltpu.VMEM((STEPS, 2) + part, jnp.bfloat16),
            pltpu.VMEM((sched_rows, 128), jnp.int32),
            pltpu.SMEM((sched_rows, 128), jnp.int32),
            pltpu.VMEM((per_dev + 2, rows + 2, ch, cols), jnp.bfloat16),
            pltpu.VMEM((per_dev + 2, rows + 2, ch, cols), jnp.bfloat16),
            pltpu.VMEM((per_dev,) + part, jnp.bfloat16),
            pltpu.VMEM((8, 8, 128), jnp.float32),
            pltpu.SemaphoreType.DMA((STEPS, 2, PARTS)),
            pltpu.SemaphoreType.DMA((STEPS, 2, PARTS)),
            pltpu.SemaphoreType.DMA,
            pltpu.SemaphoreType.DMA((2, 5)),
            pltpu.SemaphoreType.DMA((2, 5)),
            pltpu.SemaphoreType.DMA((7,)),
            pltpu.SemaphoreType.DMA((7,)),
        ],
        compiler_params=pltpu.CompilerParams(
            collective_id=0, has_side_effects=True, vmem_limit_bytes=48 * 2**20
        ),
    )(
        turned, plan_owner, plan_slot, clip_lengths[None], gain_one[None], weights[0], bias_one[None],
        gain_two[None], weights[1], bias_two[None],
    )
    return lax.cond(
        late[0, 0] > 0,
        lambda *args: general_body(*args),
        lambda *args: jnp.transpose(fast, (0, 2, 1, 3)),
        groups, plan_owner, plan_slot, clip_lengths, gain_one, weight_one, bias_one, gain_two, weight_two, bias_two,
    )


def solution(mesh):
    return jax.shard_map(
        body,
        mesh=mesh,
        in_specs=(
            P(("dp", "tm"), None, None, "space", None),
            P("dp", None),
            P("dp", None),
            P(),
            P(),
            P(),
            P(),
            P(),
            P(),
            P(),
        ),
        out_specs=P(("dp", "tm"), None, "space", None),
        check_vma=False,
    )
```

```python
import jax
import jax.numpy as jnp
from jax import lax
from jax.experimental import pallas as pl
from jax.experimental.pallas import tpu as pltpu
from jax.sharding import PartitionSpec as P

MESH = pl.DeviceIdType.MESH
STEPS = 8
LANES = 2
PARTS = 2


def shifted(value, axis, steps):
    count = lax.axis_size(axis)
    initial, last = (max(0, -steps), min(count, count - steps))
    return lax.ppermute(value, axis, [(source, source + steps) for source in range(initial, last)])


def with_halo(block, sides, width):
    for axis, dim in sides:
        count = lax.axis_size(axis)
        forward = [(i, i + 1) for i in range(count - 1)]
        backward = [(target, source) for source, target in forward]
        low = lax.ppermute(
            lax.slice_in_dim(block, block.shape[dim] - width, None, axis=dim), axis, forward
        )
        high = lax.ppermute(lax.slice_in_dim(block, 0, width, axis=dim), axis, backward)
        block = jnp.concatenate([low, block, high], axis=dim)
    return block


def normed_silu(values, gain):
    square = jnp.mean(values * values, axis=1, keepdims=True)
    return jax.nn.silu(values * lax.rsqrt(square + 1e-06) * gain[None, :, None, None])


def frame_offsets(frame_ids, clip_lengths):
    starts = jnp.cumsum(clip_lengths) - clip_lengths
    below = starts[None, :] <= frame_ids[:, None]
    latest = jnp.max(jnp.where(below, starts[None, :], 0), axis=1)
    return frame_ids - latest


def causal_conv(field, weight, keep):
    frames = field.shape[0] - 2
    width = field.shape[1]
    rows = field.shape[2] - 2
    cols = field.shape[3]
    padded = jnp.pad(field, ((0, 0), (0, 0), (0, 0), (1, 1)))
    layers = [
        padded[tap : tap + frames] * keep[:, 2 - tap][:, None, None, None] for tap in range(3)
    ]
    stacked = jnp.stack(layers, axis=1).reshape(frames, 3 * width, rows + 2, cols + 2)
    kernel = jnp.transpose(weight, (1, 2, 3, 0, 4)).reshape(3, 3, width, 3 * width)
    total = jnp.zeros((frames, width, rows, cols), jnp.float32)
    for drow in range(3):
        for dcol in range(3):
            window = stacked[:, :, drow : drow + rows, dcol : dcol + cols]
            total = total + jnp.einsum(
                "ok,fkrw->forw", kernel[drow, dcol], window, preferred_element_type=jnp.float32
            )
    return total


def general_body(
    groups,
    plan_owner,
    plan_slot,
    clip_lengths,
    gain_one,
    weight_one,
    bias_one,
    gain_two,
    weight_two,
    bias_two,
):
    owners_count = lax.axis_size("tm")
    place = lax.axis_index("tm")
    span_index = lax.axis_index("dp")
    per_dev = groups.shape[0]
    capacity = max(1, per_dev // owners_count)
    frames = per_dev * groups.shape[1]
    width = groups.shape[2]
    rows = groups.shape[3]
    cols = groups.shape[4]
    owners_all = plan_owner[0].reshape(owners_count, per_dev)
    slots_all = plan_slot[0].reshape(owners_count, per_dev)
    earlier = jnp.arange(per_dev)[:, None] > jnp.arange(per_dev)[None, :]
    same_owner = owners_all[:, :, None] == owners_all[:, None, :]
    ranks = jnp.sum(same_owner & earlier[None], axis=2)
    mine_owner = lax.dynamic_index_in_dim(owners_all, place, 0, keepdims=False)
    mine_rank = lax.dynamic_index_in_dim(ranks, place, 0, keepdims=False)
    targets = jnp.arange(owners_count, dtype=jnp.int32)[:, None, None]
    copies = jnp.arange(capacity, dtype=jnp.int32)[None, :, None]
    select = (mine_owner[None, None, :] == targets) & (mine_rank[None, None, :] == copies)
    select = select.astype(jnp.bfloat16).reshape(owners_count * capacity, per_dev)
    outgoing = jnp.dot(select, groups.reshape(per_dev, -1), preferred_element_type=jnp.float32)
    outgoing = outgoing.astype(jnp.bfloat16).reshape((owners_count * capacity,) + groups.shape[1:])
    incoming = lax.all_to_all(outgoing, "tm", split_axis=0, concat_axis=0, tiled=True)
    slot_ids = jnp.arange(per_dev, dtype=jnp.int32)[:, None, None, None]
    copy_ids = jnp.arange(capacity, dtype=jnp.int32)[None, None, :, None]
    pick = (
        (owners_all == place)[None, :, None, :]
        & (slots_all[None, :, None, :] == slot_ids)
        & (ranks[None, :, None, :] == copy_ids)
    )
    pick = (
        jnp.sum(pick.astype(jnp.int32), axis=3)
        .astype(jnp.bfloat16)
        .reshape(per_dev, owners_count * capacity)
    )
    local = jnp.dot(
        pick, incoming.reshape(owners_count * capacity, -1), preferred_element_type=jnp.float32
    )
    local = local.astype(jnp.bfloat16).reshape(frames, width, rows, cols)
    first = (span_index * owners_count + place) * frames
    frame_ids = first - 4 + jnp.arange(frames + 4, dtype=jnp.int32)
    offsets = frame_offsets(frame_ids, clip_lengths)
    keep = (offsets[:, None] >= jnp.arange(3, dtype=jnp.int32)[None, :]).astype(jnp.bfloat16)
    residual = local.astype(jnp.float32)
    hidden_one = normed_silu(residual, gain_one).astype(jnp.bfloat16)
    cache_first = shifted(hidden_one[frames - 2 :], ("dp", "tm"), 1)
    banded_one = with_halo(jnp.concatenate([cache_first, hidden_one], axis=0), (("space", 2),), 1)
    act = causal_conv(banded_one, weight_one, keep[4:]) + bias_one[None, :, None, None]
    hidden_two = normed_silu(act, gain_two).astype(jnp.bfloat16)
    cache_second = shifted(hidden_two[frames - 2 :], ("dp", "tm"), 1)
    banded_two = with_halo(jnp.concatenate([cache_second, hidden_two], axis=0), (("space", 2),), 1)
    mixed = causal_conv(banded_two, weight_two, keep[4:])
    return (residual + mixed + bias_two[None, :, None, None]).astype(jnp.bfloat16)


def column(row, size):
    down = lax.broadcasted_iota(jnp.int32, (size, size), 0)
    across = lax.broadcasted_iota(jnp.int32, (size, size), 1)
    spread = jnp.where(down == across, jnp.broadcast_to(row, (size, size)), jnp.zeros((), row.dtype))
    return jnp.sum(spread, axis=1, keepdims=True)


def plan_start(owner_ref, slot_ref, states, final, count, per_dev):
    total = count * per_dev
    shape = (total, 128)
    group = lax.broadcasted_iota(jnp.int32, shape, 0)
    lane = lax.broadcasted_iota(jnp.int32, shape, 1) & (count - 1)
    owner = jnp.broadcast_to(column(owner_ref[...], total), shape)
    place = jnp.broadcast_to(column(slot_ref[...], total), shape)
    source = group // per_dev
    entry = group - source * per_dev
    ahead = (owner - source) & (count - 1)
    forward = ahead < count // 2
    here = lane == source
    code = (group << 10) | (place << 8) | entry
    states[0] = jnp.where(here & forward, ((ahead + 1) << 16) | code, 0)
    states[1] = jnp.where(here & jnp.logical_not(forward), ((count - ahead) << 16) | code, 0)
    for s in range(per_dev):
        for row, at in ((s, count - 1), (per_dev + s, 0)):
            found = jnp.where(here & (ahead == at) & (place == s), entry, 0)
            final[pl.ds(row, 1), :] = jnp.max(found, axis=0, keepdims=True)


def plan_step(t, states, final, sched, per_dev):
    group = lax.broadcasted_iota(jnp.int32, states.shape[1:], 0)
    for way in range(2):
        state = states[way]
        arrivals = []
        for c in range(LANES):
            best = jnp.max(state, axis=0, keepdims=True)
            sched[t, pl.ds(way * LANES + c, 1), :] = best & 255
            state = jnp.where(state == best, 0, state)
            entry = per_dev + (2 * t + way) * LANES + c
            moved = jnp.where(best > 0, best - (best & 255) - (1 << 16) + entry, -1)
            moved = pltpu.roll(moved, 1 if way == 0 else 127, 1)
            left, slot = moved >> 16, (moved >> 8) & 3
            for s in range(per_dev):
                for row, hops in ((s, way), (per_dev + s, 1 - way)):
                    old = final[pl.ds(row, 1), :]
                    final[pl.ds(row, 1), :] = jnp.where((left == hops) & (slot == s), entry, old)
            arrivals.append((moved, left))
        for moved, left in arrivals:
            state = jnp.where((group == ((moved >> 10) & 63)) & (left > 0), moved, state)
        states[way] = state


def silu_norm(values, gain):
    square = jnp.mean(values * values, axis=0, keepdims=True)
    scaled = values * lax.rsqrt(square + 1e-06) * gain
    return scaled / (1.0 + jnp.exp(-scaled))


def conv_rows(field, weights, mask, at, rows):
    ch, cols = field.shape[2], field.shape[3]
    right_side = jnp.concatenate(
        [field[at : at + 3, r : r + 3].reshape(9 * ch, cols) for r in range(rows)], axis=1
    )
    sums = jnp.dot(weights * mask, right_side, preferred_element_type=jnp.float32)
    lane = lax.broadcasted_iota(jnp.int32, (ch, cols), 1)
    out = []
    for r in range(rows):
        part = sums[:, r * cols : (r + 1) * cols]
        low = jnp.where(lane == 0, 0.0, pltpu.roll(part[:ch], 1, 1))
        high = jnp.where(lane == cols - 1, 0.0, pltpu.roll(part[2 * ch :], cols - 1, 1))
        out.append(part[ch : 2 * ch] + low + high)
    return out


def block_kernel(
    groups, owner, slot, clips, gain_one, weight_one, bias_one, gain_two, weight_two, bias_two,
    out, late_out,
    pool, sending, arrived, beside, states, final, sched, sched_s, final_s, h_one, h_two, timeline, before, stage,
    late_all, send_sem, recv_sem, side_send, side_recv, sched_sem, span_send, span_recv, late_send, late_recv,
):
    spans, places, bands = lax.axis_size("dp"), lax.axis_size("tm"), lax.axis_size("space")
    dp, tm, sp = lax.axis_index("dp"), lax.axis_index("tm"), lax.axis_index("space")
    per_dev, rows, ch, cols = out.shape
    part_rows = rows * ch // PARTS
    tm_up, tm_down = lax.rem(tm + 1, places), lax.rem(tm + places - 1, places)
    sp_up, sp_down = lax.rem(sp + 1, bands), lax.rem(sp + bands - 1, bands)

    barrier = pltpu.get_barrier_semaphore()
    friends = [(dp, tm_up, sp), (dp, tm_down, sp), (dp, tm, sp_up), (dp, tm, sp_down)]
    friends += [(lax.rem(dp + k, spans), tm, sp) for k in range(1, spans)]
    for friend in friends:
        pl.semaphore_signal(barrier, inc=1, device_id=friend, device_id_type=MESH)

    def to_scalars(t):
        return pltpu.make_async_copy(sched.at[t], sched_s.at[t], sched_sem.at[0])

    def hop(t, way, c, p):
        k = (2 * t + way) * LANES + c
        return pltpu.make_async_remote_copy(
            src_ref=sending.at[k, p], dst_ref=arrived.at[k, p],
            send_sem=send_sem.at[k, p], recv_sem=recv_sem.at[k, p],
            device_id=(dp, tm_up if way == 0 else tm_down, sp), device_id_type=MESH,
        )

    def side(source, entry, p):
        return pltpu.make_async_remote_copy(
            src_ref=source, dst_ref=beside.at[entry, 1 - p],
            send_sem=side_send.at[entry, p], recv_sem=side_recv.at[entry, 1 - p],
            device_id=(dp, tm, sp_down if p == 0 else sp_up), device_id_type=MESH,
        )

    def send(t, c, p):
        for way in range(2):
            k = (2 * t + way) * LANES + c
            sending[k, p] = pool[sched_s[t, way * LANES + c, tm], p]
            hop(t, way, c, p).start()

    def receive(t, c, p):
        for way in range(2):
            k = (2 * t + way) * LANES + c
            hop(t, way, c, p).wait()
            pool[per_dev + k, p] = arrived[k, p]

    def share(t, c, p):
        for way in range(2):
            k = (2 * t + way) * LANES + c
            side(arrived.at[k, p], per_dev + k, p).start()

    plan_start(owner, slot, states, final, places, per_dev)
    plan_step(0, states, final, sched, per_dev)
    to_scalars(0).start()
    for f in range(per_dev):
        for p in range(PARTS):
            pool[f, p] = groups[f, p * part_rows : (p + 1) * part_rows]
    to_scalars(0).wait()
    pl.semaphore_wait(barrier, len(friends))

    for c in range(LANES):
        for p in range(PARTS):
            send(0, c, p)
    for f in range(per_dev):
        for p in range(PARTS):
            side(groups.at[f, pl.ds(p * part_rows, part_rows)], f, p).start()
    plan_step(1, states, final, sched, per_dev)
    to_scalars(1).start()

    def turn(t):
        to_scalars(t).wait()
        for c in range(LANES):
            for p in range(PARTS):
                receive(t - 1, c, p)
                send(t, c, p)
                share(t - 1, c, p)

    def step(t, carry):
        turn(t)
        plan_step(t + 1, states, final, sched, per_dev)
        to_scalars(t + 1).start()
        return carry

    lax.fori_loop(1, STEPS - 1, step, 0)
    turn(STEPS - 1)

    final_copy = pltpu.make_async_copy(final, final_s, sched_sem.at[1])
    final_copy.start()
    late = jnp.max(jnp.maximum(states[0], states[1]), axis=0, keepdims=True)
    late = jnp.max(late, axis=1, keepdims=True)
    late_all[0] = jnp.broadcast_to((late > 0).astype(jnp.float32), (8, 128))
    late_copies = []
    for k in range(1, spans):
        copy = pltpu.make_async_remote_copy(
            src_ref=late_all.at[0], dst_ref=late_all.at[k], send_sem=late_send.at[k - 1],
            recv_sem=late_recv.at[k - 1], device_id=(lax.rem(dp + k, spans), tm, sp), device_id_type=MESH,
        )
        copy.start()
        late_copies.append(copy)
    gain_a = column(gain_one[...], ch)
    gain_b = column(gain_two[...], ch)
    bias_a = column(bias_one[...], ch)
    bias_b = column(bias_two[...], ch)
    first = (dp * places + tm) * per_dev
    tap = lax.broadcasted_iota(jnp.int32, (1, 9 * ch), 1) // (3 * ch)
    masks = []
    for s in range(-2, per_dev):
        start, latest = jnp.int32(0), jnp.int32(0)
        for c in range(clips.shape[1]):
            latest = jnp.where(start <= first + s, start, latest)
            start = start + clips[0, c]
        masks.append((2 - tap <= first + s - latest).astype(jnp.float32).astype(jnp.bfloat16))
    final_copy.wait()
    entries = [final_s[f, tm] for f in range(2 * per_dev)]

    for c in range(LANES):
        for p in range(PARTS):
            receive(STEPS - 1, c, p)
            share(STEPS - 1, c, p)

    def to_next(k):
        return pltpu.make_async_remote_copy(
            src_ref=stage.at[k], dst_ref=before.at[k], send_sem=span_send.at[k], recv_sem=span_recv.at[k],
            device_id=(lax.rem(dp + 1, spans), tm, sp), device_id_type=MESH,
        )

    def norm_rows(f, at, values):
        for r in range(2):
            h_one[f, at + r] = silu_norm(
                values[r * ch : (r + 1) * ch].astype(jnp.float32), gain_a
            ).astype(jnp.bfloat16)

    def outside(field, low, high):
        @pl.when(sp == 0)
        def _():
            field[:, :low] = jnp.zeros((field.shape[0], low, ch, cols), field.dtype)

        @pl.when(sp == bands - 1)
        def _():
            field[:, high:] = jnp.zeros((field.shape[0], field.shape[1] - high, ch, cols), field.dtype)

    @pl.when(tm == 0)
    def _():
        for f in range(per_dev):
            for p in range(PARTS):
                stage[0, f, p] = pool[entries[f], p]
        to_next(0).start()

    for f in range(2 * per_dev):
        for p in range(PARTS):
            values = pool[entries[f], p]
            if f >= per_dev:
                timeline[f - per_dev, p] = values
            norm_rows(f, 2 + 2 * p, values)

    def side_wait(entry, carry):
        for p in range(PARTS):
            side(arrived.at[0, p], entry, p).wait_send()
            side(arrived.at[0, p], entry, 1 - p).wait_recv()
        return carry

    lax.fori_loop(0, per_dev + 2 * LANES * STEPS, side_wait, 0)

    @pl.when(tm == 0)
    def _():
        for f in range(per_dev):
            for p in range(2):
                stage[1, f, p] = beside[entries[f], p]
        to_next(1).start()

    for f in range(2 * per_dev):
        for p in range(2):
            norm_rows(f, 6 * p, beside[entries[f], p])
    outside(h_one, 2, rows + 2)

    def first_conv(j):
        for r, act in enumerate(conv_rows(h_one, weight_one[...], masks[j], j, rows + 2)):
            h_two[j, r] = silu_norm(act + bias_a, gain_b).astype(jnp.bfloat16)

    first_conv(5)
    first_conv(4)

    @pl.when(tm == 0)
    def _():
        for k in range(2):
            to_next(k).wait()
        for f in range(per_dev):
            for p in range(PARTS):
                norm_rows(f, 2 + 2 * p, before[0, f, p])
                norm_rows(f, 6 * p, before[1, f, p])
        outside(h_one, 2, rows + 2)

    for j in (3, 2, 1, 0):
        first_conv(j)
    outside(h_two, 1, rows + 1)
    for s in (3, 2, 1, 0):
        for r, mixed in enumerate(conv_rows(h_two, weight_two[...], masks[s + 2], s, rows)):
            p, at = divmod(r * ch, part_rows)
            kept = timeline[s, p, at : at + ch].astype(jnp.float32)
            out[s, r] = (kept + mixed + bias_b).astype(jnp.bfloat16)

    for copy in late_copies:
        copy.wait()
    late_out[...] = jnp.max(late_all[...], axis=0)


def fast_body(
    groups, plan_owner, plan_slot, clip_lengths, gain_one, weight_one, bias_one, gain_two, weight_two, bias_two
):
    per_dev, _, ch, rows, cols = groups.shape
    spans = lax.axis_size("dp")
    turned = jnp.transpose(groups[:, 0], (0, 2, 1, 3)).reshape(per_dev, rows * ch, cols)
    weights = [
        jnp.transpose(w, (2, 3, 0, 1, 4)).reshape(3 * ch, 9 * ch) for w in (weight_one, weight_two)
    ]
    vmem, smem = pl.BlockSpec(memory_space=pltpu.VMEM), pl.BlockSpec(memory_space=pltpu.SMEM)
    part = (PARTS, rows * ch // PARTS, cols)
    sends = 2 * LANES * STEPS
    return pl.pallas_call(
        block_kernel,
        out_shape=(
            jax.ShapeDtypeStruct((per_dev, rows, ch, cols), jnp.bfloat16),
            jax.ShapeDtypeStruct((8, 128), jnp.float32),
        ),
        in_specs=[vmem, vmem, vmem, smem] + [vmem] * 6,
        out_specs=(vmem, vmem),
        scratch_shapes=[
            pltpu.VMEM((per_dev + sends,) + part, jnp.bfloat16),
            pltpu.VMEM((sends,) + part, jnp.bfloat16),
            pltpu.VMEM((sends,) + part, jnp.bfloat16),
            pltpu.VMEM((per_dev + sends,) + part, jnp.bfloat16),
            pltpu.VMEM((2, plan_owner.shape[1], 128), jnp.int32),
            pltpu.VMEM((8, 128), jnp.int32),
            pltpu.VMEM((STEPS, 8, 128), jnp.int32),
            pltpu.SMEM((STEPS, 8, 128), jnp.int32),
            pltpu.SMEM((8, 128), jnp.int32),
            pltpu.VMEM((2 * per_dev, rows + 4, ch, cols), jnp.bfloat16),
            pltpu.VMEM((per_dev + 2, rows + 2, ch, cols), jnp.bfloat16),
            pltpu.VMEM((per_dev,) + part, jnp.bfloat16),
            pltpu.VMEM((2, per_dev) + part, jnp.bfloat16),
            pltpu.VMEM((2, per_dev) + part, jnp.bfloat16),
            pltpu.VMEM((spans, 8, 128), jnp.float32),
            pltpu.SemaphoreType.DMA((sends, PARTS)),
            pltpu.SemaphoreType.DMA((sends, PARTS)),
            pltpu.SemaphoreType.DMA((per_dev + sends, PARTS)),
            pltpu.SemaphoreType.DMA((per_dev + sends, PARTS)),
            pltpu.SemaphoreType.DMA((2,)),
            pltpu.SemaphoreType.DMA((2,)),
            pltpu.SemaphoreType.DMA((2,)),
            pltpu.SemaphoreType.DMA((spans - 1,)),
            pltpu.SemaphoreType.DMA((spans - 1,)),
        ],
        compiler_params=pltpu.CompilerParams(
            collective_id=0, has_side_effects=True, vmem_limit_bytes=48 * 2**20
        ),
    )(
        turned, plan_owner, plan_slot, clip_lengths[None], gain_one[None], weights[0], bias_one[None],
        gain_two[None], weights[1], bias_two[None],
    )


def body(*args):
    fast, late = fast_body(*args)
    return lax.cond(
        late[0, 0] > 0,
        lambda *args: general_body(*args),
        lambda *args: jnp.transpose(fast, (0, 2, 1, 3)),
        *args,
    )


def solution(mesh):
    return jax.shard_map(
        body,
        mesh=mesh,
        in_specs=(
            P(("dp", "tm"), None, None, "space", None),
            P("dp", None),
            P("dp", None),
            P(),
            P(),
            P(),
            P(),
            P(),
            P(),
            P(),
        ),
        out_specs=P(("dp", "tm"), None, "space", None),
        check_vma=False,
    )
```

```python
import jax
import jax.numpy as jnp
from jax import lax
from jax.experimental import pallas as pl
from jax.experimental.pallas import tpu as pltpu
from jax.sharding import PartitionSpec as P

MESH = pl.DeviceIdType.MESH
STEPS = 8
LANES = 2
PARTS = 2


def shifted(value, axis, steps):
    count = lax.axis_size(axis)
    initial, last = (max(0, -steps), min(count, count - steps))
    return lax.ppermute(value, axis, [(source, source + steps) for source in range(initial, last)])


def with_halo(block, sides, width):
    for axis, dim in sides:
        count = lax.axis_size(axis)
        forward = [(i, i + 1) for i in range(count - 1)]
        backward = [(target, source) for source, target in forward]
        low = lax.ppermute(
            lax.slice_in_dim(block, block.shape[dim] - width, None, axis=dim), axis, forward
        )
        high = lax.ppermute(lax.slice_in_dim(block, 0, width, axis=dim), axis, backward)
        block = jnp.concatenate([low, block, high], axis=dim)
    return block


def normed_silu(values, gain):
    square = jnp.mean(values * values, axis=1, keepdims=True)
    return jax.nn.silu(values * lax.rsqrt(square + 1e-06) * gain[None, :, None, None])


def frame_offsets(frame_ids, clip_lengths):
    starts = jnp.cumsum(clip_lengths) - clip_lengths
    below = starts[None, :] <= frame_ids[:, None]
    latest = jnp.max(jnp.where(below, starts[None, :], 0), axis=1)
    return frame_ids - latest


def causal_conv(field, weight, keep):
    frames = field.shape[0] - 2
    width = field.shape[1]
    rows = field.shape[2] - 2
    cols = field.shape[3]
    padded = jnp.pad(field, ((0, 0), (0, 0), (0, 0), (1, 1)))
    layers = [
        padded[tap : tap + frames] * keep[:, 2 - tap][:, None, None, None] for tap in range(3)
    ]
    stacked = jnp.stack(layers, axis=1).reshape(frames, 3 * width, rows + 2, cols + 2)
    kernel = jnp.transpose(weight, (1, 2, 3, 0, 4)).reshape(3, 3, width, 3 * width)
    total = jnp.zeros((frames, width, rows, cols), jnp.float32)
    for drow in range(3):
        for dcol in range(3):
            window = stacked[:, :, drow : drow + rows, dcol : dcol + cols]
            total = total + jnp.einsum(
                "ok,fkrw->forw", kernel[drow, dcol], window, preferred_element_type=jnp.float32
            )
    return total


def general_body(
    groups,
    plan_owner,
    plan_slot,
    clip_lengths,
    gain_one,
    weight_one,
    bias_one,
    gain_two,
    weight_two,
    bias_two,
):
    owners_count = lax.axis_size("tm")
    place = lax.axis_index("tm")
    span_index = lax.axis_index("dp")
    per_dev = groups.shape[0]
    capacity = max(1, per_dev // owners_count)
    frames = per_dev * groups.shape[1]
    width = groups.shape[2]
    rows = groups.shape[3]
    cols = groups.shape[4]
    owners_all = plan_owner[0].reshape(owners_count, per_dev)
    slots_all = plan_slot[0].reshape(owners_count, per_dev)
    earlier = jnp.arange(per_dev)[:, None] > jnp.arange(per_dev)[None, :]
    same_owner = owners_all[:, :, None] == owners_all[:, None, :]
    ranks = jnp.sum(same_owner & earlier[None], axis=2)
    mine_owner = lax.dynamic_index_in_dim(owners_all, place, 0, keepdims=False)
    mine_rank = lax.dynamic_index_in_dim(ranks, place, 0, keepdims=False)
    targets = jnp.arange(owners_count, dtype=jnp.int32)[:, None, None]
    copies = jnp.arange(capacity, dtype=jnp.int32)[None, :, None]
    select = (mine_owner[None, None, :] == targets) & (mine_rank[None, None, :] == copies)
    select = select.astype(jnp.bfloat16).reshape(owners_count * capacity, per_dev)
    outgoing = jnp.dot(select, groups.reshape(per_dev, -1), preferred_element_type=jnp.float32)
    outgoing = outgoing.astype(jnp.bfloat16).reshape((owners_count * capacity,) + groups.shape[1:])
    incoming = lax.all_to_all(outgoing, "tm", split_axis=0, concat_axis=0, tiled=True)
    slot_ids = jnp.arange(per_dev, dtype=jnp.int32)[:, None, None, None]
    copy_ids = jnp.arange(capacity, dtype=jnp.int32)[None, None, :, None]
    pick = (
        (owners_all == place)[None, :, None, :]
        & (slots_all[None, :, None, :] == slot_ids)
        & (ranks[None, :, None, :] == copy_ids)
    )
    pick = (
        jnp.sum(pick.astype(jnp.int32), axis=3)
        .astype(jnp.bfloat16)
        .reshape(per_dev, owners_count * capacity)
    )
    local = jnp.dot(
        pick, incoming.reshape(owners_count * capacity, -1), preferred_element_type=jnp.float32
    )
    local = local.astype(jnp.bfloat16).reshape(frames, width, rows, cols)
    first = (span_index * owners_count + place) * frames
    frame_ids = first - 4 + jnp.arange(frames + 4, dtype=jnp.int32)
    offsets = frame_offsets(frame_ids, clip_lengths)
    keep = (offsets[:, None] >= jnp.arange(3, dtype=jnp.int32)[None, :]).astype(jnp.bfloat16)
    residual = local.astype(jnp.float32)
    hidden_one = normed_silu(residual, gain_one).astype(jnp.bfloat16)
    cache_first = shifted(hidden_one[frames - 2 :], ("dp", "tm"), 1)
    banded_one = with_halo(jnp.concatenate([cache_first, hidden_one], axis=0), (("space", 2),), 1)
    act = causal_conv(banded_one, weight_one, keep[4:]) + bias_one[None, :, None, None]
    hidden_two = normed_silu(act, gain_two).astype(jnp.bfloat16)
    cache_second = shifted(hidden_two[frames - 2 :], ("dp", "tm"), 1)
    banded_two = with_halo(jnp.concatenate([cache_second, hidden_two], axis=0), (("space", 2),), 1)
    mixed = causal_conv(banded_two, weight_two, keep[4:])
    return (residual + mixed + bias_two[None, :, None, None]).astype(jnp.bfloat16)


def column(row, size):
    down = lax.broadcasted_iota(jnp.int32, (size, size), 0)
    across = lax.broadcasted_iota(jnp.int32, (size, size), 1)
    spread = jnp.where(down == across, jnp.broadcast_to(row, (size, size)), jnp.zeros((), row.dtype))
    return jnp.sum(spread, axis=1, keepdims=True)


def plan_start(owner_ref, slot_ref, states, final, count, per_dev):
    total = count * per_dev
    shape = (total, 128)
    group = lax.broadcasted_iota(jnp.int32, shape, 0)
    lane = lax.broadcasted_iota(jnp.int32, shape, 1) & (count - 1)
    owner = jnp.broadcast_to(column(owner_ref[...], total), shape)
    place = jnp.broadcast_to(column(slot_ref[...], total), shape)
    source = group // per_dev
    entry = group - source * per_dev
    ahead = (owner - source) & (count - 1)
    forward = ahead < count // 2
    here = lane == source
    code = (group << 10) | (place << 8) | entry
    states[0] = jnp.where(here & forward, ((ahead + 1) << 16) | code, 0)
    states[1] = jnp.where(here & jnp.logical_not(forward), ((count - ahead) << 16) | code, 0)
    for s in range(per_dev):
        for row, at in ((s, count - 1), (per_dev + s, 0)):
            found = jnp.where(here & (ahead == at) & (place == s), entry, 0)
            final[pl.ds(row, 1), :] = jnp.max(found, axis=0, keepdims=True)


def plan_step(t, states, final, sched, per_dev):
    group = lax.broadcasted_iota(jnp.int32, states.shape[1:], 0)
    for way in range(2):
        state = states[way]
        arrivals = []
        for c in range(LANES):
            best = jnp.max(state, axis=0, keepdims=True)
            sched[t, pl.ds(way * LANES + c, 1), :] = best & 255
            state = jnp.where(state == best, 0, state)
            entry = per_dev + (2 * t + way) * LANES + c
            moved = jnp.where(best > 0, best - (best & 255) - (1 << 16) + entry, -1)
            moved = pltpu.roll(moved, 1 if way == 0 else 127, 1)
            left, slot = moved >> 16, (moved >> 8) & 3
            for s in range(per_dev):
                for row, hops in ((s, way), (per_dev + s, 1 - way)):
                    old = final[pl.ds(row, 1), :]
                    final[pl.ds(row, 1), :] = jnp.where((left == hops) & (slot == s), entry, old)
            arrivals.append((moved, left))
        for moved, left in arrivals:
            state = jnp.where((group == ((moved >> 10) & 63)) & (left > 0), moved, state)
        states[way] = state


def silu_norm(values, gain):
    square = jnp.mean(values * values, axis=0, keepdims=True)
    scaled = values * lax.rsqrt(square + 1e-06) * gain
    return scaled / (1.0 + jnp.exp(-scaled))


def conv_rows(field, weights, mask, at, rows):
    ch, cols = field.shape[2], field.shape[3]
    right_side = jnp.concatenate(
        [field[at : at + 3, r : r + 3].reshape(9 * ch, cols) for r in range(rows)], axis=1
    )
    sums = jnp.dot(weights * mask, right_side, preferred_element_type=jnp.float32)
    lane = lax.broadcasted_iota(jnp.int32, (ch, cols), 1)
    out = []
    for r in range(rows):
        part = sums[:, r * cols : (r + 1) * cols]
        low = jnp.where(lane == 0, 0.0, pltpu.roll(part[:ch], 1, 1))
        high = jnp.where(lane == cols - 1, 0.0, pltpu.roll(part[2 * ch :], cols - 1, 1))
        out.append(part[ch : 2 * ch] + low + high)
    return out


def block_kernel(
    groups, owner, slot, clips, gain_one, weight_one, bias_one, gain_two, weight_two, bias_two,
    out, late_out,
    pool, sending, arrived, beside, beside_last, states, final, sched, sched_s, final_s, h_one, h_two, timeline, before, stage,
    late_all, before_final, before_final_s, raw, stacked, back,
    send_sem, recv_sem, side_send, side_recv, sched_sem, span_send, span_recv, late_send, late_recv, raw_sem,
):
    spans, places, bands = lax.axis_size("dp"), lax.axis_size("tm"), lax.axis_size("space")
    dp, tm, sp = lax.axis_index("dp"), lax.axis_index("tm"), lax.axis_index("space")
    per_dev, cols, ch = out.shape[0], out.shape[2], h_one.shape[2]
    rows = out.shape[1] // ch
    part_rows = rows * ch // PARTS
    tm_up, tm_down = lax.rem(tm + 1, places), lax.rem(tm + places - 1, places)
    sp_up, sp_down = lax.rem(sp + 1, bands), lax.rem(sp + bands - 1, bands)

    barrier = pltpu.get_barrier_semaphore()
    friends = [(dp, tm_up, sp), (dp, tm_down, sp), (dp, tm, sp_up), (dp, tm, sp_down)]
    friends += [(lax.rem(dp + k, spans), tm, sp) for k in range(1, spans)]
    dp_next = jnp.where(tm == places - 1, lax.rem(dp + 1, spans), dp)
    dp_prev = jnp.where(tm == 0, lax.rem(dp + spans - 1, spans), dp)
    friends += [(dp_next, tm_up, sp), (dp_prev, tm_down, sp)]
    for friend in friends:
        pl.semaphore_signal(barrier, inc=1, device_id=friend, device_id_type=MESH)

    def to_scalars(t):
        return pltpu.make_async_copy(sched.at[t], sched_s.at[t], sched_sem.at[0])

    last = per_dev + 2 * LANES * (STEPS - 1)

    def hop(t, c, p, way):
        ends = isinstance(t, int) and t == STEPS - 1 and way == 0
        at = (t * LANES + c, p) if way is None else (t * LANES + c, p, way)
        return pltpu.make_async_remote_copy(
            src_ref=sending.at[at], dst_ref=arrived.at[at],
            send_sem=send_sem.at[lax.rem(t, 2), c, p], recv_sem=recv_sem.at[t, c, p],
            device_id=(dp_next if ends else dp, tm_down if way == 1 else tm_up, sp), device_id_type=MESH,
        )

    def side(source, entry, p):
        block = entry // (2 * LANES)
        here = beside_last.at[entry - last] if isinstance(entry, int) and entry >= last else beside.at[entry]
        return pltpu.make_async_remote_copy(
            src_ref=source, dst_ref=here.at[1 - p], send_sem=side_send.at[block], recv_sem=side_recv.at[block],
            device_id=(dp, tm, sp_down if p == 0 else sp_up), device_id_type=MESH,
        )

    def side_wait(block):
        every = beside.at[pl.ds(0, 2 * LANES)]
        pltpu.make_async_remote_copy(
            src_ref=every, dst_ref=beside_last if isinstance(block, int) and block == STEPS else beside.at[
                pl.ds(2 * LANES * block, 2 * LANES)
            ],
            send_sem=side_send.at[block], recv_sem=side_recv.at[block],
            device_id=(dp, tm, sp_up), device_id_type=MESH,
        ).wait()

    def send(t, c, p):
        for way in range(2):
            sending[t * LANES + c, p, way] = pool[sched_s[t, way * LANES + c, tm], p]
            hop(t, c, p, way).start()

    def receive(t, c, p):
        hop(t, c, p, None).wait()
        for way in range(2):
            pool[per_dev + (2 * t + way) * LANES + c, p] = arrived[t * LANES + c, p, way]

    def share(t, c, p):
        for way in range(2):
            side(arrived.at[t * LANES + c, p, way], per_dev + (2 * t + way) * LANES + c, p).start()

    raws = [pltpu.make_async_copy(w, raw.at[k], raw_sem.at[k]) for k, w in enumerate((weight_one, weight_two))]
    for copy in raws:
        copy.start()
    plan_start(owner, slot, states, final, places, per_dev)
    plan_step(0, states, final, sched, per_dev)
    to_scalars(0).start()
    size = rows * ch
    down = lax.broadcasted_iota(jnp.int32, (size, size), 0)
    across = lax.broadcasted_iota(jnp.int32, (size, size), 1)
    turn_rows = ((across & (rows - 1)) * ch + across // rows == down).astype(jnp.float32).astype(jnp.bfloat16)
    mine = jnp.dot(
        turn_rows, jnp.concatenate([groups[f] for f in range(per_dev)], axis=1), preferred_element_type=jnp.float32
    ).astype(jnp.bfloat16)
    for f in range(per_dev):
        for p in range(PARTS):
            pool[f, p] = mine[p * part_rows : (p + 1) * part_rows, f * cols : (f + 1) * cols]
    to_scalars(0).wait()
    pl.semaphore_wait(barrier, len(friends))

    for c in range(LANES):
        for p in range(PARTS):
            send(0, c, p)
    for f in range(per_dev):
        for p in range(PARTS):
            side(pool.at[f, p], f, p).start()
    plan_step(1, states, final, sched, per_dev)
    to_scalars(1).start()
    for k, copy in enumerate(raws):
        copy.wait()
        stacked[k] = jnp.concatenate([raw[k, j] for j in range(9)], axis=1)
    back[...] = ((down & (rows - 1)) * ch + down // rows == across).astype(jnp.float32).astype(jnp.bfloat16)

    def turn(t):
        to_scalars(t).wait()
        for c in range(LANES):
            for p in range(PARTS):
                receive(t - 1, c, p)
                send(t, c, p)
                share(t - 1, c, p)
        side_wait(t - 1)

    def step(t, carry):
        turn(t)
        plan_step(t + 1, states, final, sched, per_dev)
        to_scalars(t + 1).start()
        return carry

    lax.fori_loop(1, STEPS - 1, step, 0)
    final_copy = pltpu.make_async_copy(final, final_s, sched_sem.at[1])
    final_copy.start()
    turn(STEPS - 1)

    final_copy.wait()
    entries = [final_s[f, tm] for f in range(2 * per_dev)]

    span_copies = []
    for j, part in enumerate((pl.ds(1, PARTS), 0, 3)):
        span_copies.append(pltpu.make_async_remote_copy(
            src_ref=stage.at[:, part], dst_ref=before.at[pl.ds(0, per_dev), part],
            send_sem=span_send.at[j], recv_sem=span_recv.at[j],
            device_id=(lax.rem(dp + 1, spans), tm, sp), device_id_type=MESH,
        ))
    final_next = pltpu.make_async_remote_copy(
        src_ref=final, dst_ref=before_final, send_sem=span_send.at[3], recv_sem=span_recv.at[3],
        device_id=(lax.rem(dp + 1, spans), tm, sp), device_id_type=MESH,
    )

    @pl.when(tm == 0)
    def _():
        for f in range(per_dev):
            entry = jnp.where(entries[f] >= last, 0, entries[f])
            for p in range(PARTS):
                stage[f, 1 + p] = pool[entry, p]
        span_copies[0].start()
        final_next.start()

    late = jnp.max(jnp.maximum(states[0], states[1]), axis=0, keepdims=True)
    late = jnp.max(late, axis=1, keepdims=True)
    late_all[0] = jnp.broadcast_to((late > 0).astype(jnp.float32), (8, 128))
    for k in range(1, spans):
        copy = pltpu.make_async_remote_copy(
            src_ref=late_all.at[0], dst_ref=late_all.at[k], send_sem=late_send, recv_sem=late_recv,
            device_id=(lax.rem(dp + k, spans), tm, sp), device_id_type=MESH,
        )
        copy.start()
    gain_a = column(gain_one[...], ch)
    gain_b = column(gain_two[...], ch)
    bias_a = column(bias_one[...], ch)
    bias_b = column(bias_two[...], ch)
    first = (dp * places + tm) * per_dev
    tap = lax.broadcasted_iota(jnp.int32, (1, 9 * ch), 1) // (3 * ch)
    masks = []
    for s in range(-2, per_dev):
        start, latest = jnp.int32(0), jnp.int32(0)
        for c in range(clips.shape[1]):
            latest = jnp.where(start <= first + s, start, latest)
            start = start + clips[0, c]
        masks.append((2 - tap <= first + s - latest).astype(jnp.float32).astype(jnp.bfloat16))
    for c in range(LANES):
        for p in range(PARTS):
            receive(STEPS - 1, c, p)
            share(STEPS - 1, c, p)
        if c == 0:
            side_wait(STEPS - 1)

            @pl.when(tm == 0)
            def _():
                for f in range(per_dev):
                    entry = jnp.where(entries[f] >= last, 0, entries[f])
                    for p in range(2):
                        stage[f, 3 * p] = beside[entry, p]
                for copy in span_copies[1:]:
                    copy.start()

    def norm_rows(f, at, values):
        for r in range(2):
            h_one[f, at + r] = silu_norm(
                values[r * ch : (r + 1) * ch].astype(jnp.float32), gain_a
            ).astype(jnp.bfloat16)

    def outside(field, low, high):
        @pl.when(sp == 0)
        def _():
            field[:, :low] = jnp.zeros((field.shape[0], low, ch, cols), field.dtype)

        @pl.when(sp == bands - 1)
        def _():
            field[:, high:] = jnp.zeros((field.shape[0], field.shape[1] - high, ch, cols), field.dtype)

    for f in range(2 * per_dev):
        for p in range(PARTS):
            values = pool[entries[f], p]
            if f >= per_dev:
                timeline[f - per_dev, p] = values
            norm_rows(f, 2 + 2 * p, values)

    side_wait(STEPS)

    for k in range(2 * LANES):
        for p in range(2):
            beside[last + k, p] = beside_last[k, p]
    for f in range(2 * per_dev):
        for p in range(2):
            norm_rows(f, 6 * p, beside[entries[f], p])
    outside(h_one, 2, rows + 2)

    def first_conv(j):
        for r, act in enumerate(conv_rows(h_one, stacked[0], masks[j], j, rows + 2)):
            h_two[j, r] = silu_norm(act + bias_a, gain_b).astype(jnp.bfloat16)

    first_conv(5)
    first_conv(4)

    @pl.when(tm == 0)
    def _():
        final_next.wait()
        move = pltpu.make_async_copy(before_final, before_final_s, sched_sem.at[1])
        move.start()
        for c in range(LANES):
            for p in range(2):
                before[per_dev + c, 1 + p] = pool[last + c, p]
                before[per_dev + c, 3 * p] = beside_last[c, p]
        for copy in span_copies:
            copy.wait()
        move.wait()
        for f in range(per_dev):
            entry = before_final_s[f, 0]
            entry = jnp.where(entry >= last, per_dev + jnp.minimum(entry - last, LANES - 1), f)
            for q in range(4):
                norm_rows(f, 2 * q, before[entry, q])
        outside(h_one, 2, rows + 2)

    for j in (3, 2, 1, 0):
        first_conv(j)
    outside(h_two, 1, rows + 1)
    for pair in ((3, 2), (1, 0)):
        ready = []
        for s in pair:
            mixed = jnp.concatenate(conv_rows(h_two, stacked[1], masks[s + 2], s, rows), axis=0)
            kept = timeline[s].reshape(size, cols).astype(jnp.float32)
            bias = jnp.concatenate([bias_b] * rows, axis=0)
            ready.append((kept + mixed + bias).astype(jnp.bfloat16))
        turned = jnp.dot(back[...], jnp.concatenate(ready, axis=1), preferred_element_type=jnp.float32)
        for k, s in enumerate(pair):
            out[s] = turned[:, k * cols : (k + 1) * cols].astype(jnp.bfloat16)

    others = late_all.at[pl.ds(1, spans - 1)]
    pltpu.make_async_remote_copy(
        src_ref=others, dst_ref=others, send_sem=late_send, recv_sem=late_recv,
        device_id=(lax.rem(dp + 1, spans), tm, sp), device_id_type=MESH,
    ).wait()
    late_out[...] = jnp.max(late_all[...], axis=0)


def fast_body(
    groups, plan_owner, plan_slot, clip_lengths, gain_one, weight_one, bias_one, gain_two, weight_two, bias_two
):
    per_dev, _, ch, rows, cols = groups.shape
    spans = lax.axis_size("dp")
    vmem, smem = pl.BlockSpec(memory_space=pltpu.VMEM), pl.BlockSpec(memory_space=pltpu.SMEM)
    whole = pl.BlockSpec(memory_space=pl.ANY)
    part = (PARTS, rows * ch // PARTS, cols)
    sends = 2 * LANES * STEPS
    return pl.pallas_call(
        block_kernel,
        out_shape=(
            jax.ShapeDtypeStruct((per_dev, rows * ch, cols), jnp.bfloat16),
            jax.ShapeDtypeStruct((8, 128), jnp.float32),
        ),
        in_specs=[vmem, vmem, vmem, smem, vmem, whole, vmem, vmem, whole, vmem],
        out_specs=(vmem, vmem),
        scratch_shapes=[
            pltpu.VMEM((per_dev + sends,) + part, jnp.bfloat16),
            pltpu.VMEM((STEPS * LANES, PARTS, 2) + part[1:], jnp.bfloat16),
            pltpu.VMEM((STEPS * LANES, PARTS, 2) + part[1:], jnp.bfloat16),
            pltpu.VMEM((per_dev + sends,) + part, jnp.bfloat16),
            pltpu.VMEM((2 * LANES,) + part, jnp.bfloat16),
            pltpu.VMEM((2, plan_owner.shape[1], 128), jnp.int32),
            pltpu.VMEM((8, 128), jnp.int32),
            pltpu.VMEM((STEPS, 8, 128), jnp.int32),
            pltpu.SMEM((STEPS, 8, 128), jnp.int32),
            pltpu.SMEM((8, 128), jnp.int32),
            pltpu.VMEM((2 * per_dev, rows + 4, ch, cols), jnp.bfloat16),
            pltpu.VMEM((per_dev + 2, rows + 2, ch, cols), jnp.bfloat16),
            pltpu.VMEM((per_dev,) + part, jnp.bfloat16),
            pltpu.VMEM((per_dev + LANES, 4) + part[1:], jnp.bfloat16),
            pltpu.VMEM((per_dev, 4) + part[1:], jnp.bfloat16),
            pltpu.VMEM((spans, 8, 128), jnp.float32),
            pltpu.VMEM((8, 128), jnp.int32),
            pltpu.SMEM((8, 128), jnp.int32),
            pltpu.VMEM((2, 9, 3 * ch, ch), jnp.bfloat16),
            pltpu.VMEM((2, 3 * ch, 9 * ch), jnp.bfloat16),
            pltpu.VMEM((rows * ch, rows * ch), jnp.bfloat16),
            pltpu.SemaphoreType.DMA((2, LANES, PARTS)),
            pltpu.SemaphoreType.DMA((STEPS, LANES, PARTS)),
            pltpu.SemaphoreType.DMA((STEPS + 1,)),
            pltpu.SemaphoreType.DMA((STEPS + 1,)),
            pltpu.SemaphoreType.DMA((2,)),
            pltpu.SemaphoreType.DMA((4,)),
            pltpu.SemaphoreType.DMA((4,)),
            pltpu.SemaphoreType.DMA,
            pltpu.SemaphoreType.DMA,
            pltpu.SemaphoreType.DMA((2,)),
        ],
        compiler_params=pltpu.CompilerParams(
            collective_id=0, has_side_effects=True, vmem_limit_bytes=48 * 2**20
        ),
    )(
        groups.reshape(per_dev, ch * rows, cols), plan_owner, plan_slot, clip_lengths[None], gain_one[None],
        weight_one.reshape(9, 3 * ch, ch), bias_one[None], gain_two[None], weight_two.reshape(9, 3 * ch, ch),
        bias_two[None],
    )


def body(*args):
    fast, late = fast_body(*args)
    return lax.cond(
        late[0, 0] > 0,
        lambda *args: general_body(*args),
        lambda *args: fast.reshape(args[0].shape[:1] + args[0].shape[2:]),
        *args,
    )


def solution(mesh):
    return jax.shard_map(
        body,
        mesh=mesh,
        in_specs=(
            P(("dp", "tm"), None, None, "space", None),
            P("dp", None),
            P("dp", None),
            P(),
            P(),
            P(),
            P(),
            P(),
            P(),
            P(),
        ),
        out_specs=P(("dp", "tm"), None, "space", None),
        check_vma=False,
    )
```

```python
import jax
import jax.numpy as jnp
from jax import lax
from jax.experimental import pallas as pl
from jax.experimental.pallas import tpu as pltpu
from jax.sharding import PartitionSpec as P

MESH = pl.DeviceIdType.MESH
STEPS = 8
LANES = 2
PARTS = 2


def shifted(value, axis, steps):
    count = lax.axis_size(axis)
    initial, last = (max(0, -steps), min(count, count - steps))
    return lax.ppermute(value, axis, [(source, source + steps) for source in range(initial, last)])


def with_halo(block, sides, width):
    for axis, dim in sides:
        count = lax.axis_size(axis)
        forward = [(i, i + 1) for i in range(count - 1)]
        backward = [(target, source) for source, target in forward]
        low = lax.ppermute(
            lax.slice_in_dim(block, block.shape[dim] - width, None, axis=dim), axis, forward
        )
        high = lax.ppermute(lax.slice_in_dim(block, 0, width, axis=dim), axis, backward)
        block = jnp.concatenate([low, block, high], axis=dim)
    return block


def normed_silu(values, gain):
    square = jnp.mean(values * values, axis=1, keepdims=True)
    return jax.nn.silu(values * lax.rsqrt(square + 1e-06) * gain[None, :, None, None])


def frame_offsets(frame_ids, clip_lengths):
    starts = jnp.cumsum(clip_lengths) - clip_lengths
    below = starts[None, :] <= frame_ids[:, None]
    latest = jnp.max(jnp.where(below, starts[None, :], 0), axis=1)
    return frame_ids - latest


def causal_conv(field, weight, keep):
    frames = field.shape[0] - 2
    width = field.shape[1]
    rows = field.shape[2] - 2
    cols = field.shape[3]
    padded = jnp.pad(field, ((0, 0), (0, 0), (0, 0), (1, 1)))
    layers = [
        padded[tap : tap + frames] * keep[:, 2 - tap][:, None, None, None] for tap in range(3)
    ]
    stacked = jnp.stack(layers, axis=1).reshape(frames, 3 * width, rows + 2, cols + 2)
    kernel = jnp.transpose(weight, (1, 2, 3, 0, 4)).reshape(3, 3, width, 3 * width)
    total = jnp.zeros((frames, width, rows, cols), jnp.float32)
    for drow in range(3):
        for dcol in range(3):
            window = stacked[:, :, drow : drow + rows, dcol : dcol + cols]
            total = total + jnp.einsum(
                "ok,fkrw->forw", kernel[drow, dcol], window, preferred_element_type=jnp.float32
            )
    return total


def general_body(
    groups,
    plan_owner,
    plan_slot,
    clip_lengths,
    gain_one,
    weight_one,
    bias_one,
    gain_two,
    weight_two,
    bias_two,
):
    owners_count = lax.axis_size("tm")
    place = lax.axis_index("tm")
    span_index = lax.axis_index("dp")
    per_dev = groups.shape[0]
    capacity = max(1, per_dev // owners_count)
    frames = per_dev * groups.shape[1]
    width = groups.shape[2]
    rows = groups.shape[3]
    cols = groups.shape[4]
    owners_all = plan_owner[0].reshape(owners_count, per_dev)
    slots_all = plan_slot[0].reshape(owners_count, per_dev)
    earlier = jnp.arange(per_dev)[:, None] > jnp.arange(per_dev)[None, :]
    same_owner = owners_all[:, :, None] == owners_all[:, None, :]
    ranks = jnp.sum(same_owner & earlier[None], axis=2)
    mine_owner = lax.dynamic_index_in_dim(owners_all, place, 0, keepdims=False)
    mine_rank = lax.dynamic_index_in_dim(ranks, place, 0, keepdims=False)
    targets = jnp.arange(owners_count, dtype=jnp.int32)[:, None, None]
    copies = jnp.arange(capacity, dtype=jnp.int32)[None, :, None]
    select = (mine_owner[None, None, :] == targets) & (mine_rank[None, None, :] == copies)
    select = select.astype(jnp.bfloat16).reshape(owners_count * capacity, per_dev)
    outgoing = jnp.dot(select, groups.reshape(per_dev, -1), preferred_element_type=jnp.float32)
    outgoing = outgoing.astype(jnp.bfloat16).reshape((owners_count * capacity,) + groups.shape[1:])
    incoming = lax.all_to_all(outgoing, "tm", split_axis=0, concat_axis=0, tiled=True)
    slot_ids = jnp.arange(per_dev, dtype=jnp.int32)[:, None, None, None]
    copy_ids = jnp.arange(capacity, dtype=jnp.int32)[None, None, :, None]
    pick = (
        (owners_all == place)[None, :, None, :]
        & (slots_all[None, :, None, :] == slot_ids)
        & (ranks[None, :, None, :] == copy_ids)
    )
    pick = (
        jnp.sum(pick.astype(jnp.int32), axis=3)
        .astype(jnp.bfloat16)
        .reshape(per_dev, owners_count * capacity)
    )
    local = jnp.dot(
        pick, incoming.reshape(owners_count * capacity, -1), preferred_element_type=jnp.float32
    )
    local = local.astype(jnp.bfloat16).reshape(frames, width, rows, cols)
    first = (span_index * owners_count + place) * frames
    frame_ids = first - 4 + jnp.arange(frames + 4, dtype=jnp.int32)
    offsets = frame_offsets(frame_ids, clip_lengths)
    keep = (offsets[:, None] >= jnp.arange(3, dtype=jnp.int32)[None, :]).astype(jnp.bfloat16)
    residual = local.astype(jnp.float32)
    hidden_one = normed_silu(residual, gain_one).astype(jnp.bfloat16)
    cache_first = shifted(hidden_one[frames - 2 :], ("dp", "tm"), 1)
    banded_one = with_halo(jnp.concatenate([cache_first, hidden_one], axis=0), (("space", 2),), 1)
    act = causal_conv(banded_one, weight_one, keep[4:]) + bias_one[None, :, None, None]
    hidden_two = normed_silu(act, gain_two).astype(jnp.bfloat16)
    cache_second = shifted(hidden_two[frames - 2 :], ("dp", "tm"), 1)
    banded_two = with_halo(jnp.concatenate([cache_second, hidden_two], axis=0), (("space", 2),), 1)
    mixed = causal_conv(banded_two, weight_two, keep[4:])
    return (residual + mixed + bias_two[None, :, None, None]).astype(jnp.bfloat16)


def column(row, size):
    down = lax.broadcasted_iota(jnp.int32, (size, size), 0)
    across = lax.broadcasted_iota(jnp.int32, (size, size), 1)
    spread = jnp.where(down == across, jnp.broadcast_to(row, (size, size)), jnp.zeros((), row.dtype))
    return jnp.sum(spread, axis=1, keepdims=True)


def plan_start(owner_ref, slot_ref, states, final, count, per_dev):
    total = count * per_dev
    shape = (total, 128)
    group = lax.broadcasted_iota(jnp.int32, shape, 0)
    lane = lax.broadcasted_iota(jnp.int32, shape, 1) & (count - 1)
    owner = jnp.broadcast_to(column(owner_ref[...], total), shape)
    place = jnp.broadcast_to(column(slot_ref[...], total), shape)
    source = group // per_dev
    entry = group - source * per_dev
    ahead = (owner - source) & (count - 1)
    forward = ahead < count // 2
    here = lane == source
    code = (group << 10) | (place << 8) | entry
    states[0] = jnp.where(here & forward, ((ahead + 1) << 16) | code, 0)
    states[1] = jnp.where(here & jnp.logical_not(forward), ((count - ahead) << 16) | code, 0)
    for s in range(per_dev):
        for row, at in ((s, count - 1), (per_dev + s, 0)):
            found = jnp.where(here & (ahead == at) & (place == s), entry, 0)
            final[pl.ds(row, 1), :] = jnp.max(found, axis=0, keepdims=True)


def plan_step(t, states, final, sched, per_dev):
    group = lax.broadcasted_iota(jnp.int32, states.shape[1:], 0)
    for way in range(2):
        state = states[way]
        arrivals = []
        for c in range(LANES):
            best = jnp.max(state, axis=0, keepdims=True)
            sched[t, pl.ds(way * LANES + c, 1), :] = best & 255
            state = jnp.where(state == best, 0, state)
            entry = per_dev + (2 * t + way) * LANES + c
            moved = jnp.where(best > 0, best - (best & 255) - (1 << 16) + entry, -1)
            moved = pltpu.roll(moved, 1 if way == 0 else 127, 1)
            left, slot = moved >> 16, (moved >> 8) & 3
            for s in range(per_dev):
                for row, hops in ((s, way), (per_dev + s, 1 - way)):
                    old = final[pl.ds(row, 1), :]
                    final[pl.ds(row, 1), :] = jnp.where((left == hops) & (slot == s), entry, old)
            arrivals.append((moved, left))
        for moved, left in arrivals:
            state = jnp.where((group == ((moved >> 10) & 63)) & (left > 0), moved, state)
        states[way] = state


def silu_norm(values, gain):
    square = jnp.mean(values * values, axis=0, keepdims=True)
    scaled = values * lax.rsqrt(square + 1e-06) * gain
    return scaled / (1.0 + jnp.exp(-scaled))


def conv_rows(field, weights, mask, at, lines):
    ch, cols = field.shape[2], field.shape[3]
    right_side = jnp.concatenate(
        [field[at : at + 3, r : r + 3].reshape(9 * ch, cols) for r in lines], axis=1
    )
    sums = jnp.dot(weights * mask, right_side, preferred_element_type=jnp.float32)
    lane = lax.broadcasted_iota(jnp.int32, (ch, cols), 1)
    out = []
    for r in range(len(lines)):
        part = sums[:, r * cols : (r + 1) * cols]
        low = jnp.where(lane == 0, 0.0, pltpu.roll(part[:ch], 1, 1))
        high = jnp.where(lane == cols - 1, 0.0, pltpu.roll(part[2 * ch :], cols - 1, 1))
        out.append(part[ch : 2 * ch] + low + high)
    return out


def block_kernel(
    groups, owner, slot, clips, gain_one, weight_one, bias_one, gain_two, weight_two, bias_two,
    out, late_out,
    pool, sending, arrived, beside, beside_mid, beside_last, states, final, sched, sched_s, final_s, h_one, h_two, timeline, before, stage,
    late_all, before_final, before_final_s, raw, stacked, back,
    send_sem, recv_sem, side_send, side_recv, sched_sem, span_send, span_recv, late_send, late_recv, raw_sem,
):
    spans, places, bands = lax.axis_size("dp"), lax.axis_size("tm"), lax.axis_size("space")
    dp, tm, sp = lax.axis_index("dp"), lax.axis_index("tm"), lax.axis_index("space")
    per_dev, cols, ch = out.shape[0], out.shape[2], h_one.shape[2]
    rows = out.shape[1] // ch
    part_rows = rows * ch // PARTS
    tm_up, tm_down = lax.rem(tm + 1, places), lax.rem(tm + places - 1, places)
    sp_up, sp_down = lax.rem(sp + 1, bands), lax.rem(sp + bands - 1, bands)

    barrier = pltpu.get_barrier_semaphore()
    friends = [(dp, tm_up, sp), (dp, tm_down, sp), (dp, tm, sp_up), (dp, tm, sp_down)]
    friends += [(lax.rem(dp + k, spans), tm, sp) for k in range(1, spans)]
    dp_next = jnp.where(tm == places - 1, lax.rem(dp + 1, spans), dp)
    dp_prev = jnp.where(tm == 0, lax.rem(dp + spans - 1, spans), dp)
    friends += [(dp_next, tm_up, sp), (dp_prev, tm_down, sp)]
    for friend in friends:
        pl.semaphore_signal(barrier, inc=1, device_id=friend, device_id_type=MESH)

    def to_scalars(t):
        return pltpu.make_async_copy(sched.at[t], sched_s.at[t], sched_sem.at[0])

    last = per_dev + 2 * LANES * (STEPS - 1)
    mid = last - 2 * LANES

    def hop(t, c, p, way):
        ends = isinstance(t, int) and t == STEPS - 1 and way == 0
        at = (t * LANES + c, p) if way is None else (t * LANES + c, p, way)
        return pltpu.make_async_remote_copy(
            src_ref=sending.at[at], dst_ref=arrived.at[at],
            send_sem=send_sem.at[lax.rem(t, 2), c, p], recv_sem=recv_sem.at[t, c, p],
            device_id=(dp_next if ends else dp, tm_down if way == 1 else tm_up, sp), device_id_type=MESH,
        )

    def side(source, entry, p):
        block = entry // (2 * LANES)
        if isinstance(entry, int) and entry >= mid:
            here = beside_last.at[entry - last] if entry >= last else beside_mid.at[entry - mid]
        else:
            here = beside.at[entry]
        return pltpu.make_async_remote_copy(
            src_ref=source, dst_ref=here.at[1 - p], send_sem=side_send.at[block], recv_sem=side_recv.at[block],
            device_id=(dp, tm, sp_down if p == 0 else sp_up), device_id_type=MESH,
        )

    def side_wait(block):
        every = beside.at[pl.ds(0, 2 * LANES)]
        if isinstance(block, int) and block >= STEPS - 1:
            here = beside_last if block == STEPS else beside_mid
        else:
            here = beside.at[pl.ds(2 * LANES * block, 2 * LANES)]
        pltpu.make_async_remote_copy(
            src_ref=every, dst_ref=here,
            send_sem=side_send.at[block], recv_sem=side_recv.at[block],
            device_id=(dp, tm, sp_up), device_id_type=MESH,
        ).wait()

    def send(t, c, p):
        for way in range(2):
            sending[t * LANES + c, p, way] = pool[sched_s[t, way * LANES + c, tm], p]
            hop(t, c, p, way).start()

    def receive(t, c, p):
        hop(t, c, p, None).wait()
        for way in range(2):
            pool[per_dev + (2 * t + way) * LANES + c, p] = arrived[t * LANES + c, p, way]

    def share(t, c, p):
        for way in range(2):
            side(arrived.at[t * LANES + c, p, way], per_dev + (2 * t + way) * LANES + c, p).start()

    raws = [pltpu.make_async_copy(w, raw.at[k], raw_sem.at[k]) for k, w in enumerate((weight_one, weight_two))]
    for copy in raws:
        copy.start()
    plan_start(owner, slot, states, final, places, per_dev)
    plan_step(0, states, final, sched, per_dev)
    to_scalars(0).start()
    size = rows * ch
    down = lax.broadcasted_iota(jnp.int32, (size, size), 0)
    across = lax.broadcasted_iota(jnp.int32, (size, size), 1)
    turn_rows = ((across & (rows - 1)) * ch + across // rows == down).astype(jnp.float32).astype(jnp.bfloat16)
    mine = jnp.dot(
        turn_rows, jnp.concatenate([groups[f] for f in range(per_dev)], axis=1), preferred_element_type=jnp.float32
    ).astype(jnp.bfloat16)
    for f in range(per_dev):
        for p in range(PARTS):
            pool[f, p] = mine[p * part_rows : (p + 1) * part_rows, f * cols : (f + 1) * cols]
    to_scalars(0).wait()
    pl.semaphore_wait(barrier, len(friends))

    for c in range(LANES):
        for p in range(PARTS):
            send(0, c, p)
    for f in range(per_dev):
        for p in range(PARTS):
            side(pool.at[f, p], f, p).start()
    plan_step(1, states, final, sched, per_dev)
    to_scalars(1).start()
    for k, copy in enumerate(raws):
        copy.wait()
        stacked[k] = jnp.concatenate([raw[k, j] for j in range(9)], axis=1)
    back[...] = ((down & (rows - 1)) * ch + down // rows == across).astype(jnp.float32).astype(jnp.bfloat16)

    def turn(t):
        to_scalars(t).wait()
        for c in range(LANES):
            for p in range(PARTS):
                receive(t - 1, c, p)
                send(t, c, p)
                share(t - 1, c, p)
        side_wait(t - 1)

    def step(t, carry):
        turn(t)
        plan_step(t + 1, states, final, sched, per_dev)
        to_scalars(t + 1).start()
        return carry

    lax.fori_loop(1, STEPS - 1, step, 0)
    final_copy = pltpu.make_async_copy(final, final_s, sched_sem.at[1])
    final_copy.start()
    final_copy.wait()
    entries = [final_s[f, tm] for f in range(2 * per_dev)]

    def among(found):
        one = two = jnp.int32(0)
        for entry in found:
            one = jnp.maximum(one, jnp.where((entry >= mid) & (entry < last), entry, 0))
        for entry in found:
            two = jnp.maximum(two, jnp.where((entry >= mid) & (entry < last) & (entry != one), entry, 0))
        return jnp.maximum(one, mid), jnp.maximum(two, mid)

    early = [jnp.where(entries[f] >= mid, 0, entries[f]) for f in range(per_dev)]
    later = among(entries[:per_dev])
    span_copies = []
    for j, (at, part) in enumerate((
        (pl.ds(0, per_dev), pl.ds(1, PARTS)), (pl.ds(per_dev, 2), pl.ds(1, PARTS)),
        (pl.ds(0, per_dev), 0), (pl.ds(0, per_dev), 3), (pl.ds(per_dev, 2), 0), (pl.ds(per_dev, 2), 3),
    )):
        span_copies.append(pltpu.make_async_remote_copy(
            src_ref=stage.at[at, part], dst_ref=before.at[at, part],
            send_sem=span_send.at[j], recv_sem=span_recv.at[j],
            device_id=(lax.rem(dp + 1, spans), tm, sp), device_id_type=MESH,
        ))
    final_next = pltpu.make_async_remote_copy(
        src_ref=final, dst_ref=before_final, send_sem=span_send.at[6], recv_sem=span_recv.at[6],
        device_id=(lax.rem(dp + 1, spans), tm, sp), device_id_type=MESH,
    )

    @pl.when(tm == 0)
    def _():
        for f in range(per_dev):
            for p in range(PARTS):
                stage[f, 1 + p] = pool[early[f], p]
        span_copies[0].start()
        final_next.start()

    turn(STEPS - 1)

    @pl.when(tm == 0)
    def _():
        for k in range(2):
            for p in range(PARTS):
                stage[per_dev + k, 1 + p] = pool[later[k], p]
        span_copies[1].start()
        for f in range(per_dev):
            for p in range(2):
                stage[f, 3 * p] = beside[early[f], p]
        span_copies[2].start()
        span_copies[3].start()

    late = jnp.max(jnp.maximum(states[0], states[1]), axis=0, keepdims=True)
    many = ((final[:per_dev] >= mid) & (final[:per_dev] < last)).astype(jnp.int32)
    many = jnp.sum(many, axis=0, keepdims=True) - 2
    many = jnp.where(lax.broadcasted_iota(jnp.int32, (1, 128), 1) == 0, many, 0)
    late = jnp.max(jnp.maximum(late, many), axis=1, keepdims=True)
    late_all[0] = jnp.broadcast_to((late > 0).astype(jnp.float32), (8, 128))
    for k in range(1, spans):
        copy = pltpu.make_async_remote_copy(
            src_ref=late_all.at[0], dst_ref=late_all.at[k], send_sem=late_send, recv_sem=late_recv,
            device_id=(lax.rem(dp + k, spans), tm, sp), device_id_type=MESH,
        )
        copy.start()
    gain_a = column(gain_one[...], ch)
    gain_b = column(gain_two[...], ch)
    bias_a = column(bias_one[...], ch)
    bias_b = column(bias_two[...], ch)
    first = (dp * places + tm) * per_dev
    tap = lax.broadcasted_iota(jnp.int32, (1, 9 * ch), 1) // (3 * ch)
    masks = []
    for s in range(-2, per_dev):
        start, latest = jnp.int32(0), jnp.int32(0)
        for c in range(clips.shape[1]):
            latest = jnp.where(start <= first + s, start, latest)
            start = start + clips[0, c]
        masks.append((2 - tap <= first + s - latest).astype(jnp.float32).astype(jnp.bfloat16))
    for c in range(LANES):
        for p in range(PARTS):
            receive(STEPS - 1, c, p)
            share(STEPS - 1, c, p)
        if c == 0:
            side_wait(STEPS - 1)

            @pl.when(tm == 0)
            def _():
                for k in range(2):
                    for p in range(2):
                        stage[per_dev + k, 3 * p] = beside_mid[later[k] - mid, p]
                span_copies[4].start()
                span_copies[5].start()

    def norm_rows(f, at, values):
        for r in range(2):
            h_one[f, at + r] = silu_norm(
                values[r * ch : (r + 1) * ch].astype(jnp.float32), gain_a
            ).astype(jnp.bfloat16)

    def outside(field, low, high):
        @pl.when(sp == 0)
        def _():
            field[:, :low] = jnp.zeros((field.shape[0], low, ch, cols), field.dtype)

        @pl.when(sp == bands - 1)
        def _():
            field[:, high:] = jnp.zeros((field.shape[0], field.shape[1] - high, ch, cols), field.dtype)

    for f in range(2 * per_dev):
        for p in range(PARTS):
            values = pool[entries[f], p]
            if f >= per_dev:
                timeline[f - per_dev, p] = values
            norm_rows(f, 2 + 2 * p, values)

    inner, outer = tuple(range(2, rows)), (0, 1, rows, rows + 1)

    def first_conv(j, lines):
        for r, act in zip(lines, conv_rows(h_one, stacked[0], masks[j], j, lines)):
            h_two[j, r] = silu_norm(act + bias_a, gain_b).astype(jnp.bfloat16)

    for j in (5, 4):
        first_conv(j, inner)
    others = late_all.at[pl.ds(1, spans - 1)]
    pltpu.make_async_remote_copy(
        src_ref=others, dst_ref=others, send_sem=late_send, recv_sem=late_recv,
        device_id=(lax.rem(dp + 1, spans), tm, sp), device_id_type=MESH,
    ).wait()
    late_out[...] = jnp.max(late_all[...], axis=0).astype(jnp.int32)
    side_wait(STEPS)

    for k in range(2 * LANES):
        for p in range(2):
            beside[mid + k, p] = beside_mid[k, p]
            beside[last + k, p] = beside_last[k, p]
    for f in range(2 * per_dev):
        for p in range(2):
            norm_rows(f, 6 * p, beside[entries[f], p])
    outside(h_one, 2, rows + 2)

    first_conv(5, outer)
    first_conv(4, outer)

    @pl.when(tm == 0)
    def _():
        final_next.wait()
        move = pltpu.make_async_copy(before_final, before_final_s, sched_sem.at[1])
        move.start()
        for c in range(LANES):
            for p in range(2):
                before[per_dev + 2 + c, 1 + p] = pool[last + c, p]
                before[per_dev + 2 + c, 3 * p] = beside_last[c, p]
        for copy in span_copies:
            copy.wait()
        move.wait()
        found = [before_final_s[f, 0] for f in range(per_dev)]
        one, _ = among(found)
        for f in range(per_dev):
            entry = jnp.where(found[f] == one, per_dev, per_dev + 1)
            entry = jnp.where(found[f] >= mid, entry, f)
            entry = jnp.where(found[f] >= last, per_dev + 2 + jnp.minimum(found[f] - last, LANES - 1), entry)
            for q in range(4):
                norm_rows(f, 2 * q, before[entry, q])
        outside(h_one, 2, rows + 2)

    for j in (3, 2, 1, 0):
        first_conv(j, range(rows + 2))
    outside(h_two, 1, rows + 1)
    for pair in ((3, 2), (1, 0)):
        ready = []
        for s in pair:
            mixed = jnp.concatenate(conv_rows(h_two, stacked[1], masks[s + 2], s, range(rows)), axis=0)
            kept = timeline[s].reshape(size, cols).astype(jnp.float32)
            bias = jnp.concatenate([bias_b] * rows, axis=0)
            ready.append((kept + mixed + bias).astype(jnp.bfloat16))
        turned = jnp.dot(back[...], jnp.concatenate(ready, axis=1), preferred_element_type=jnp.float32)
        for k, s in enumerate(pair):
            out[s] = turned[:, k * cols : (k + 1) * cols].astype(jnp.bfloat16)


def fast_body(
    groups, plan_owner, plan_slot, clip_lengths, gain_one, weight_one, bias_one, gain_two, weight_two, bias_two
):
    per_dev, _, ch, rows, cols = groups.shape
    spans = lax.axis_size("dp")
    vmem, smem = pl.BlockSpec(memory_space=pltpu.VMEM), pl.BlockSpec(memory_space=pltpu.SMEM)
    whole = pl.BlockSpec(memory_space=pl.ANY)
    part = (PARTS, rows * ch // PARTS, cols)
    sends = 2 * LANES * STEPS
    return pl.pallas_call(
        block_kernel,
        out_shape=(
            jax.ShapeDtypeStruct((per_dev, rows * ch, cols), jnp.bfloat16),
            jax.ShapeDtypeStruct((8, 128), jnp.int32),
        ),
        in_specs=[vmem, vmem, vmem, smem, vmem, whole, vmem, vmem, whole, vmem],
        out_specs=(vmem, vmem),
        scratch_shapes=[
            pltpu.VMEM((per_dev + sends,) + part, jnp.bfloat16),
            pltpu.VMEM((STEPS * LANES, PARTS, 2) + part[1:], jnp.bfloat16),
            pltpu.VMEM((STEPS * LANES, PARTS, 2) + part[1:], jnp.bfloat16),
            pltpu.VMEM((per_dev + sends,) + part, jnp.bfloat16),
            pltpu.VMEM((2 * LANES,) + part, jnp.bfloat16),
            pltpu.VMEM((2 * LANES,) + part, jnp.bfloat16),
            pltpu.VMEM((2, plan_owner.shape[1], 128), jnp.int32),
            pltpu.VMEM((8, 128), jnp.int32),
            pltpu.VMEM((STEPS, 8, 128), jnp.int32),
            pltpu.SMEM((STEPS, 8, 128), jnp.int32),
            pltpu.SMEM((8, 128), jnp.int32),
            pltpu.VMEM((2 * per_dev, rows + 4, ch, cols), jnp.bfloat16),
            pltpu.VMEM((per_dev + 2, rows + 2, ch, cols), jnp.bfloat16),
            pltpu.VMEM((per_dev,) + part, jnp.bfloat16),
            pltpu.VMEM((per_dev + 2 + LANES, 4) + part[1:], jnp.bfloat16),
            pltpu.VMEM((per_dev + 2, 4) + part[1:], jnp.bfloat16),
            pltpu.VMEM((spans, 8, 128), jnp.float32),
            pltpu.VMEM((8, 128), jnp.int32),
            pltpu.SMEM((8, 128), jnp.int32),
            pltpu.VMEM((2, 9, 3 * ch, ch), jnp.bfloat16),
            pltpu.VMEM((2, 3 * ch, 9 * ch), jnp.bfloat16),
            pltpu.VMEM((rows * ch, rows * ch), jnp.bfloat16),
            pltpu.SemaphoreType.DMA((2, LANES, PARTS)),
            pltpu.SemaphoreType.DMA((STEPS, LANES, PARTS)),
            pltpu.SemaphoreType.DMA((STEPS + 1,)),
            pltpu.SemaphoreType.DMA((STEPS + 1,)),
            pltpu.SemaphoreType.DMA((2,)),
            pltpu.SemaphoreType.DMA((7,)),
            pltpu.SemaphoreType.DMA((7,)),
            pltpu.SemaphoreType.DMA,
            pltpu.SemaphoreType.DMA,
            pltpu.SemaphoreType.DMA((2,)),
        ],
        compiler_params=pltpu.CompilerParams(
            collective_id=0, has_side_effects=True, vmem_limit_bytes=48 * 2**20
        ),
    )(
        groups.reshape(per_dev, ch * rows, cols), plan_owner, plan_slot, clip_lengths[None], gain_one[None],
        weight_one.reshape(9, 3 * ch, ch), bias_one[None], gain_two[None], weight_two.reshape(9, 3 * ch, ch),
        bias_two[None],
    )


def body(*args):
    fast, late = fast_body(*args)
    return lax.switch(
        late[0, 0],
        (lambda *args: fast.reshape(args[0].shape[:1] + args[0].shape[2:]), lambda *args: general_body(*args)),
        *args,
    )


def solution(mesh):
    return jax.shard_map(
        body,
        mesh=mesh,
        in_specs=(
            P(("dp", "tm"), None, None, "space", None),
            P("dp", None),
            P("dp", None),
            P(),
            P(),
            P(),
            P(),
            P(),
            P(),
            P(),
        ),
        out_specs=P(("dp", "tm"), None, "space", None),
        check_vma=False,
    )
```

```python
import jax
import jax.numpy as jnp
from jax import lax
from jax.experimental import pallas as pl
from jax.experimental.pallas import tpu as pltpu
from jax.sharding import PartitionSpec as P

MESH = pl.DeviceIdType.MESH
STEPS = 8
LANES = 2
PARTS = 2


def shifted(value, axis, steps):
    count = lax.axis_size(axis)
    initial, last = (max(0, -steps), min(count, count - steps))
    return lax.ppermute(value, axis, [(source, source + steps) for source in range(initial, last)])


def with_halo(block, sides, width):
    for axis, dim in sides:
        count = lax.axis_size(axis)
        forward = [(i, i + 1) for i in range(count - 1)]
        backward = [(target, source) for source, target in forward]
        low = lax.ppermute(
            lax.slice_in_dim(block, block.shape[dim] - width, None, axis=dim), axis, forward
        )
        high = lax.ppermute(lax.slice_in_dim(block, 0, width, axis=dim), axis, backward)
        block = jnp.concatenate([low, block, high], axis=dim)
    return block


def normed_silu(values, gain):
    square = jnp.mean(values * values, axis=1, keepdims=True)
    return jax.nn.silu(values * lax.rsqrt(square + 1e-06) * gain[None, :, None, None])


def frame_offsets(frame_ids, clip_lengths):
    starts = jnp.cumsum(clip_lengths) - clip_lengths
    below = starts[None, :] <= frame_ids[:, None]
    latest = jnp.max(jnp.where(below, starts[None, :], 0), axis=1)
    return frame_ids - latest


def causal_conv(field, weight, keep):
    frames = field.shape[0] - 2
    width = field.shape[1]
    rows = field.shape[2] - 2
    cols = field.shape[3]
    padded = jnp.pad(field, ((0, 0), (0, 0), (0, 0), (1, 1)))
    layers = [
        padded[tap : tap + frames] * keep[:, 2 - tap][:, None, None, None] for tap in range(3)
    ]
    stacked = jnp.stack(layers, axis=1).reshape(frames, 3 * width, rows + 2, cols + 2)
    kernel = jnp.transpose(weight, (1, 2, 3, 0, 4)).reshape(3, 3, width, 3 * width)
    total = jnp.zeros((frames, width, rows, cols), jnp.float32)
    for drow in range(3):
        for dcol in range(3):
            window = stacked[:, :, drow : drow + rows, dcol : dcol + cols]
            total = total + jnp.einsum(
                "ok,fkrw->forw", kernel[drow, dcol], window, preferred_element_type=jnp.float32
            )
    return total


def general_body(
    groups,
    plan_owner,
    plan_slot,
    clip_lengths,
    gain_one,
    weight_one,
    bias_one,
    gain_two,
    weight_two,
    bias_two,
):
    owners_count = lax.axis_size("tm")
    place = lax.axis_index("tm")
    span_index = lax.axis_index("dp")
    per_dev = groups.shape[0]
    capacity = max(1, per_dev // owners_count)
    frames = per_dev * groups.shape[1]
    width = groups.shape[2]
    rows = groups.shape[3]
    cols = groups.shape[4]
    owners_all = plan_owner[0].reshape(owners_count, per_dev)
    slots_all = plan_slot[0].reshape(owners_count, per_dev)
    earlier = jnp.arange(per_dev)[:, None] > jnp.arange(per_dev)[None, :]
    same_owner = owners_all[:, :, None] == owners_all[:, None, :]
    ranks = jnp.sum(same_owner & earlier[None], axis=2)
    mine_owner = lax.dynamic_index_in_dim(owners_all, place, 0, keepdims=False)
    mine_rank = lax.dynamic_index_in_dim(ranks, place, 0, keepdims=False)
    targets = jnp.arange(owners_count, dtype=jnp.int32)[:, None, None]
    copies = jnp.arange(capacity, dtype=jnp.int32)[None, :, None]
    select = (mine_owner[None, None, :] == targets) & (mine_rank[None, None, :] == copies)
    select = select.astype(jnp.bfloat16).reshape(owners_count * capacity, per_dev)
    outgoing = jnp.dot(select, groups.reshape(per_dev, -1), preferred_element_type=jnp.float32)
    outgoing = outgoing.astype(jnp.bfloat16).reshape((owners_count * capacity,) + groups.shape[1:])
    incoming = lax.all_to_all(outgoing, "tm", split_axis=0, concat_axis=0, tiled=True)
    slot_ids = jnp.arange(per_dev, dtype=jnp.int32)[:, None, None, None]
    copy_ids = jnp.arange(capacity, dtype=jnp.int32)[None, None, :, None]
    pick = (
        (owners_all == place)[None, :, None, :]
        & (slots_all[None, :, None, :] == slot_ids)
        & (ranks[None, :, None, :] == copy_ids)
    )
    pick = (
        jnp.sum(pick.astype(jnp.int32), axis=3)
        .astype(jnp.bfloat16)
        .reshape(per_dev, owners_count * capacity)
    )
    local = jnp.dot(
        pick, incoming.reshape(owners_count * capacity, -1), preferred_element_type=jnp.float32
    )
    local = local.astype(jnp.bfloat16).reshape(frames, width, rows, cols)
    first = (span_index * owners_count + place) * frames
    frame_ids = first - 4 + jnp.arange(frames + 4, dtype=jnp.int32)
    offsets = frame_offsets(frame_ids, clip_lengths)
    keep = (offsets[:, None] >= jnp.arange(3, dtype=jnp.int32)[None, :]).astype(jnp.bfloat16)
    residual = local.astype(jnp.float32)
    hidden_one = normed_silu(residual, gain_one).astype(jnp.bfloat16)
    cache_first = shifted(hidden_one[frames - 2 :], ("dp", "tm"), 1)
    banded_one = with_halo(jnp.concatenate([cache_first, hidden_one], axis=0), (("space", 2),), 1)
    act = causal_conv(banded_one, weight_one, keep[4:]) + bias_one[None, :, None, None]
    hidden_two = normed_silu(act, gain_two).astype(jnp.bfloat16)
    cache_second = shifted(hidden_two[frames - 2 :], ("dp", "tm"), 1)
    banded_two = with_halo(jnp.concatenate([cache_second, hidden_two], axis=0), (("space", 2),), 1)
    mixed = causal_conv(banded_two, weight_two, keep[4:])
    return (residual + mixed + bias_two[None, :, None, None]).astype(jnp.bfloat16)


def column(row, size):
    down = lax.broadcasted_iota(jnp.int32, (size, size), 0)
    across = lax.broadcasted_iota(jnp.int32, (size, size), 1)
    spread = jnp.where(down == across, jnp.broadcast_to(row, (size, size)), jnp.zeros((), row.dtype))
    return jnp.sum(spread, axis=1, keepdims=True)


def plan_start(owner_ref, slot_ref, states, final, count, per_dev):
    total = count * per_dev
    shape = (total, 128)
    group = lax.broadcasted_iota(jnp.int32, shape, 0)
    lane = lax.broadcasted_iota(jnp.int32, shape, 1) & (count - 1)
    owner = jnp.broadcast_to(column(owner_ref[...], total), shape)
    place = jnp.broadcast_to(column(slot_ref[...], total), shape)
    source = group // per_dev
    entry = group - source * per_dev
    ahead = (owner - source) & (count - 1)
    forward = ahead < count // 2
    here = lane == source
    code = (group << 10) | (place << 8) | entry
    states[0] = jnp.where(here & forward, ((ahead + 1) << 16) | code, 0)
    states[1] = jnp.where(here & jnp.logical_not(forward), ((count - ahead) << 16) | code, 0)
    for s in range(per_dev):
        for row, at in ((s, count - 1), (per_dev + s, 0)):
            found = jnp.where(here & (ahead == at) & (place == s), entry, 0)
            final[pl.ds(row, 1), :] = jnp.max(found, axis=0, keepdims=True)


def plan_step(t, states, final, sched, per_dev):
    group = lax.broadcasted_iota(jnp.int32, states.shape[1:], 0)
    for way in range(2):
        state = states[way]
        arrivals = []
        for c in range(LANES):
            best = jnp.max(state, axis=0, keepdims=True)
            sched[t, pl.ds(way * LANES + c, 1), :] = best & 255
            state = jnp.where(state == best, 0, state)
            entry = per_dev + (2 * t + way) * LANES + c
            moved = jnp.where(best > 0, best - (best & 255) - (1 << 16) + entry, -1)
            moved = pltpu.roll(moved, 1 if way == 0 else 127, 1)
            left, slot = moved >> 16, (moved >> 8) & 3
            for s in range(per_dev):
                for row, hops in ((s, way), (per_dev + s, 1 - way)):
                    old = final[pl.ds(row, 1), :]
                    final[pl.ds(row, 1), :] = jnp.where((left == hops) & (slot == s), entry, old)
            arrivals.append((moved, left))
        for moved, left in arrivals:
            state = jnp.where((group == ((moved >> 10) & 63)) & (left > 0), moved, state)
        states[way] = state


def silu_norm(values, gain):
    square = jnp.mean(values * values, axis=0, keepdims=True)
    scaled = values * lax.rsqrt(square + 1e-06) * gain
    return scaled / (1.0 + jnp.exp(-scaled))


def conv_rows(field, weights, mask, at, lines):
    ch, cols = field.shape[2], field.shape[3]
    right_side = jnp.concatenate(
        [field[at : at + 3, r : r + 3].reshape(9 * ch, cols) for r in lines], axis=1
    )
    sums = jnp.dot(weights * mask, right_side, preferred_element_type=jnp.float32)
    lane = lax.broadcasted_iota(jnp.int32, (ch, cols), 1)
    out = []
    for r in range(len(lines)):
        part = sums[:, r * cols : (r + 1) * cols]
        low = jnp.where(lane == 0, 0.0, pltpu.roll(part[:ch], 1, 1))
        high = jnp.where(lane == cols - 1, 0.0, pltpu.roll(part[2 * ch :], cols - 1, 1))
        out.append(part[ch : 2 * ch] + low + high)
    return out


def block_kernel(
    groups, owner, slot, clips, gain_one, weight_one, bias_one, gain_two, weight_two, bias_two,
    out, late_out,
    pool, sending, arrived, beside, beside_last, states, final, sched, sched_s, final_s, h_one, h_two, timeline, before, stage,
    late_all, before_final, before_final_s, raw, stacked, back,
    send_sem, recv_sem, side_send, side_recv, sched_sem, span_send, span_recv, late_send, late_recv, raw_sem,
):
    spans, places, bands = lax.axis_size("dp"), lax.axis_size("tm"), lax.axis_size("space")
    dp, tm, sp = lax.axis_index("dp"), lax.axis_index("tm"), lax.axis_index("space")
    per_dev, cols, ch = out.shape[0], out.shape[2], h_one.shape[2]
    rows = out.shape[1] // ch
    part_rows = rows * ch // PARTS
    tm_up, tm_down = lax.rem(tm + 1, places), lax.rem(tm + places - 1, places)
    sp_up, sp_down = lax.rem(sp + 1, bands), lax.rem(sp + bands - 1, bands)

    barrier = pltpu.get_barrier_semaphore()
    friends = [(dp, tm_up, sp), (dp, tm_down, sp), (dp, tm, sp_up), (dp, tm, sp_down)]
    friends += [(lax.rem(dp + k, spans), tm, sp) for k in range(1, spans)]
    dp_next = jnp.where(tm == places - 1, lax.rem(dp + 1, spans), dp)
    dp_prev = jnp.where(tm == 0, lax.rem(dp + spans - 1, spans), dp)
    friends += [(dp_next, tm_up, sp), (dp_prev, tm_down, sp)]
    for friend in friends:
        pl.semaphore_signal(barrier, inc=1, device_id=friend, device_id_type=MESH)

    def to_scalars(t):
        return pltpu.make_async_copy(sched.at[t], sched_s.at[t], sched_sem.at[0])

    last = per_dev + 2 * LANES * (STEPS - 1)

    def hop(t, c, p, way):
        ends = isinstance(t, int) and t == STEPS - 1 and way == 0
        at = (t * LANES + c, p) if way is None else (t * LANES + c, p, way)
        return pltpu.make_async_remote_copy(
            src_ref=sending.at[at], dst_ref=arrived.at[at],
            send_sem=send_sem.at[lax.rem(t, 2), c, p], recv_sem=recv_sem.at[t, c, p],
            device_id=(dp_next if ends else dp, tm_down if way == 1 else tm_up, sp), device_id_type=MESH,
        )

    def side(source, entry, p):
        block = entry // (2 * LANES)
        here = beside_last.at[entry - last] if isinstance(entry, int) and entry >= last else beside.at[entry]
        return pltpu.make_async_remote_copy(
            src_ref=source, dst_ref=here.at[1 - p], send_sem=side_send.at[block], recv_sem=side_recv.at[block],
            device_id=(dp, tm, sp_down if p == 0 else sp_up), device_id_type=MESH,
        )

    def side_wait(block):
        every = beside.at[pl.ds(0, 2 * LANES)]
        pltpu.make_async_remote_copy(
            src_ref=every, dst_ref=beside_last if isinstance(block, int) and block == STEPS else beside.at[
                pl.ds(2 * LANES * block, 2 * LANES)
            ],
            send_sem=side_send.at[block], recv_sem=side_recv.at[block],
            device_id=(dp, tm, sp_up), device_id_type=MESH,
        ).wait()

    def send(t, c, p):
        for way in range(2):
            sending[t * LANES + c, p, way] = pool[sched_s[t, way * LANES + c, tm], p]
            hop(t, c, p, way).start()

    def receive(t, c, p):
        hop(t, c, p, None).wait()
        for way in range(2):
            pool[per_dev + (2 * t + way) * LANES + c, p] = arrived[t * LANES + c, p, way]

    def share(t, c, p):
        for way in range(2):
            side(arrived.at[t * LANES + c, p, way], per_dev + (2 * t + way) * LANES + c, p).start()

    raws = [pltpu.make_async_copy(w, raw.at[k], raw_sem.at[k]) for k, w in enumerate((weight_one, weight_two))]
    for copy in raws:
        copy.start()
    plan_start(owner, slot, states, final, places, per_dev)
    plan_step(0, states, final, sched, per_dev)
    to_scalars(0).start()
    size = rows * ch
    down = lax.broadcasted_iota(jnp.int32, (size, size), 0)
    across = lax.broadcasted_iota(jnp.int32, (size, size), 1)
    turn_rows = ((across & (rows - 1)) * ch + across // rows == down).astype(jnp.float32).astype(jnp.bfloat16)
    mine = jnp.dot(
        turn_rows, jnp.concatenate([groups[f] for f in range(per_dev)], axis=1), preferred_element_type=jnp.float32
    ).astype(jnp.bfloat16)
    for f in range(per_dev):
        for p in range(PARTS):
            pool[f, p] = mine[p * part_rows : (p + 1) * part_rows, f * cols : (f + 1) * cols]
    to_scalars(0).wait()
    pl.semaphore_wait(barrier, len(friends))

    for c in range(LANES):
        for p in range(PARTS):
            send(0, c, p)
    for f in range(per_dev):
        for p in range(PARTS):
            side(pool.at[f, p], f, p).start()
    plan_step(1, states, final, sched, per_dev)
    to_scalars(1).start()
    for k, copy in enumerate(raws):
        copy.wait()
        stacked[k] = jnp.concatenate([raw[k, j] for j in range(9)], axis=1)
    back[...] = ((down & (rows - 1)) * ch + down // rows == across).astype(jnp.float32).astype(jnp.bfloat16)

    def turn(t):
        to_scalars(t).wait()
        for c in range(LANES):
            for p in range(PARTS):
                receive(t - 1, c, p)
                send(t, c, p)
                share(t - 1, c, p)
        side_wait(t - 1)

    def step(t, carry):
        turn(t)
        plan_step(t + 1, states, final, sched, per_dev)
        to_scalars(t + 1).start()
        return carry

    lax.fori_loop(1, STEPS - 1, step, 0)
    final_copy = pltpu.make_async_copy(final, final_s, sched_sem.at[1])
    final_copy.start()
    turn(STEPS - 1)

    final_copy.wait()
    entries = [final_s[f, tm] for f in range(2 * per_dev)]

    span_copies = []
    for j, part in enumerate((pl.ds(1, PARTS), 0, 3)):
        span_copies.append(pltpu.make_async_remote_copy(
            src_ref=stage.at[:, part], dst_ref=before.at[pl.ds(0, per_dev), part],
            send_sem=span_send.at[j], recv_sem=span_recv.at[j],
            device_id=(lax.rem(dp + 1, spans), tm, sp), device_id_type=MESH,
        ))
    final_next = pltpu.make_async_remote_copy(
        src_ref=final, dst_ref=before_final, send_sem=span_send.at[3], recv_sem=span_recv.at[3],
        device_id=(lax.rem(dp + 1, spans), tm, sp), device_id_type=MESH,
    )

    @pl.when(tm == 0)
    def _():
        for f in range(per_dev):
            entry = jnp.where(entries[f] >= last, 0, entries[f])
            for p in range(PARTS):
                stage[f, 1 + p] = pool[entry, p]
        span_copies[0].start()
        final_next.start()

    late = jnp.max(jnp.maximum(states[0], states[1]), axis=0, keepdims=True)
    late = jnp.max(late, axis=1, keepdims=True)
    late_all[0] = jnp.broadcast_to((late > 0).astype(jnp.float32), (8, 128))
    for k in range(1, spans):
        copy = pltpu.make_async_remote_copy(
            src_ref=late_all.at[0], dst_ref=late_all.at[k], send_sem=late_send, recv_sem=late_recv,
            device_id=(lax.rem(dp + k, spans), tm, sp), device_id_type=MESH,
        )
        copy.start()
    gain_a = column(gain_one[...], ch)
    gain_b = column(gain_two[...], ch)
    bias_a = column(bias_one[...], ch)
    bias_b = column(bias_two[...], ch)
    first = (dp * places + tm) * per_dev
    tap = lax.broadcasted_iota(jnp.int32, (1, 9 * ch), 1) // (3 * ch)
    masks = []
    for s in range(-2, per_dev):
        start, latest = jnp.int32(0), jnp.int32(0)
        for c in range(clips.shape[1]):
            latest = jnp.where(start <= first + s, start, latest)
            start = start + clips[0, c]
        masks.append((2 - tap <= first + s - latest).astype(jnp.float32).astype(jnp.bfloat16))
    for c in range(LANES):
        for p in range(PARTS):
            receive(STEPS - 1, c, p)
            share(STEPS - 1, c, p)
        if c == 0:
            side_wait(STEPS - 1)

            @pl.when(tm == 0)
            def _():
                for f in range(per_dev):
                    entry = jnp.where(entries[f] >= last, 0, entries[f])
                    for p in range(2):
                        stage[f, 3 * p] = beside[entry, p]
                for copy in span_copies[1:]:
                    copy.start()

    def norm_rows(f, at, values):
        for r in range(2):
            h_one[f, at + r] = silu_norm(
                values[r * ch : (r + 1) * ch].astype(jnp.float32), gain_a
            ).astype(jnp.bfloat16)

    def outside(field, low, high):
        @pl.when(sp == 0)
        def _():
            field[:, :low] = jnp.zeros((field.shape[0], low, ch, cols), field.dtype)

        @pl.when(sp == bands - 1)
        def _():
            field[:, high:] = jnp.zeros((field.shape[0], field.shape[1] - high, ch, cols), field.dtype)

    for f in range(2 * per_dev):
        for p in range(PARTS):
            values = pool[entries[f], p]
            if f >= per_dev:
                timeline[f - per_dev, p] = values
            norm_rows(f, 2 + 2 * p, values)

    inner, outer = tuple(range(2, rows)), (0, 1, rows, rows + 1)

    def first_conv(j, lines):
        for r, act in zip(lines, conv_rows(h_one, stacked[0], masks[j], j, lines)):
            h_two[j, r] = silu_norm(act + bias_a, gain_b).astype(jnp.bfloat16)

    for j in (5, 4):
        first_conv(j, inner)
    others = late_all.at[pl.ds(1, spans - 1)]
    pltpu.make_async_remote_copy(
        src_ref=others, dst_ref=others, send_sem=late_send, recv_sem=late_recv,
        device_id=(lax.rem(dp + 1, spans), tm, sp), device_id_type=MESH,
    ).wait()
    late_out[...] = jnp.max(late_all[...], axis=0).astype(jnp.int32)
    side_wait(STEPS)

    for k in range(2 * LANES):
        for p in range(2):
            beside[last + k, p] = beside_last[k, p]
    for f in range(2 * per_dev):
        for p in range(2):
            norm_rows(f, 6 * p, beside[entries[f], p])
    outside(h_one, 2, rows + 2)

    first_conv(5, outer)
    first_conv(4, outer)

    @pl.when(tm == 0)
    def _():
        final_next.wait()
        move = pltpu.make_async_copy(before_final, before_final_s, sched_sem.at[1])
        move.start()
        for c in range(LANES):
            for p in range(2):
                before[per_dev + c, 1 + p] = pool[last + c, p]
                before[per_dev + c, 3 * p] = beside_last[c, p]
        for copy in span_copies:
            copy.wait()
        move.wait()
        for f in range(per_dev):
            entry = before_final_s[f, 0]
            entry = jnp.where(entry >= last, per_dev + jnp.minimum(entry - last, LANES - 1), f)
            for q in range(4):
                norm_rows(f, 2 * q, before[entry, q])
        outside(h_one, 2, rows + 2)

    for j in (3, 2, 1, 0):
        first_conv(j, range(rows + 2))
    outside(h_two, 1, rows + 1)
    for pair in ((3, 2), (1, 0)):
        ready = []
        for s in pair:
            mixed = jnp.concatenate(conv_rows(h_two, stacked[1], masks[s + 2], s, range(rows)), axis=0)
            kept = timeline[s].reshape(size, cols).astype(jnp.float32)
            bias = jnp.concatenate([bias_b] * rows, axis=0)
            ready.append((kept + mixed + bias).astype(jnp.bfloat16))
        turned = jnp.dot(back[...], jnp.concatenate(ready, axis=1), preferred_element_type=jnp.float32)
        for k, s in enumerate(pair):
            out[s] = turned[:, k * cols : (k + 1) * cols].astype(jnp.bfloat16)


def fast_body(
    groups, plan_owner, plan_slot, clip_lengths, gain_one, weight_one, bias_one, gain_two, weight_two, bias_two
):
    per_dev, _, ch, rows, cols = groups.shape
    spans = lax.axis_size("dp")
    vmem, smem = pl.BlockSpec(memory_space=pltpu.VMEM), pl.BlockSpec(memory_space=pltpu.SMEM)
    whole = pl.BlockSpec(memory_space=pl.ANY)
    part = (PARTS, rows * ch // PARTS, cols)
    sends = 2 * LANES * STEPS
    return pl.pallas_call(
        block_kernel,
        out_shape=(
            jax.ShapeDtypeStruct((per_dev, rows * ch, cols), jnp.bfloat16),
            jax.ShapeDtypeStruct((8, 128), jnp.int32),
        ),
        in_specs=[vmem, vmem, vmem, smem, vmem, whole, vmem, vmem, whole, vmem],
        out_specs=(vmem, vmem),
        scratch_shapes=[
            pltpu.VMEM((per_dev + sends,) + part, jnp.bfloat16),
            pltpu.VMEM((STEPS * LANES, PARTS, 2) + part[1:], jnp.bfloat16),
            pltpu.VMEM((STEPS * LANES, PARTS, 2) + part[1:], jnp.bfloat16),
            pltpu.VMEM((per_dev + sends,) + part, jnp.bfloat16),
            pltpu.VMEM((2 * LANES,) + part, jnp.bfloat16),
            pltpu.VMEM((2, plan_owner.shape[1], 128), jnp.int32),
            pltpu.VMEM((8, 128), jnp.int32),
            pltpu.VMEM((STEPS, 8, 128), jnp.int32),
            pltpu.SMEM((STEPS, 8, 128), jnp.int32),
            pltpu.SMEM((8, 128), jnp.int32),
            pltpu.VMEM((2 * per_dev, rows + 4, ch, cols), jnp.bfloat16),
            pltpu.VMEM((per_dev + 2, rows + 2, ch, cols), jnp.bfloat16),
            pltpu.VMEM((per_dev,) + part, jnp.bfloat16),
            pltpu.VMEM((per_dev + LANES, 4) + part[1:], jnp.bfloat16),
            pltpu.VMEM((per_dev, 4) + part[1:], jnp.bfloat16),
            pltpu.VMEM((spans, 8, 128), jnp.float32),
            pltpu.VMEM((8, 128), jnp.int32),
            pltpu.SMEM((8, 128), jnp.int32),
            pltpu.VMEM((2, 9, 3 * ch, ch), jnp.bfloat16),
            pltpu.VMEM((2, 3 * ch, 9 * ch), jnp.bfloat16),
            pltpu.VMEM((rows * ch, rows * ch), jnp.bfloat16),
            pltpu.SemaphoreType.DMA((2, LANES, PARTS)),
            pltpu.SemaphoreType.DMA((STEPS, LANES, PARTS)),
            pltpu.SemaphoreType.DMA((STEPS + 1,)),
            pltpu.SemaphoreType.DMA((STEPS + 1,)),
            pltpu.SemaphoreType.DMA((2,)),
            pltpu.SemaphoreType.DMA((4,)),
            pltpu.SemaphoreType.DMA((4,)),
            pltpu.SemaphoreType.DMA,
            pltpu.SemaphoreType.DMA,
            pltpu.SemaphoreType.DMA((2,)),
        ],
        compiler_params=pltpu.CompilerParams(
            collective_id=0, has_side_effects=True, vmem_limit_bytes=48 * 2**20
        ),
    )(
        groups.reshape(per_dev, ch * rows, cols), plan_owner, plan_slot, clip_lengths[None], gain_one[None],
        weight_one.reshape(9, 3 * ch, ch), bias_one[None], gain_two[None], weight_two.reshape(9, 3 * ch, ch),
        bias_two[None],
    )


def body(*args):
    fast, late = fast_body(*args)
    return lax.switch(
        late[0, 0],
        (lambda *args: fast.reshape(args[0].shape[:1] + args[0].shape[2:]), lambda *args: general_body(*args)),
        *args,
    )


def solution(mesh):
    return jax.shard_map(
        body,
        mesh=mesh,
        in_specs=(
            P(("dp", "tm"), None, None, "space", None),
            P("dp", None),
            P("dp", None),
            P(),
            P(),
            P(),
            P(),
            P(),
            P(),
            P(),
        ),
        out_specs=P(("dp", "tm"), None, "space", None),
        check_vma=False,
    )
```
